32 devices in a mesh: dev: 8 (over y, x, core), ha: 4 (over z).
Axes of the slice: x: 2, y: 2, z: 4, core: 2. Of those that a mesh axis runs over, the one named last changes fastest.
Arguments:
- volume: bfloat16 [4, 64, 64, 512], P(None, 'dev', 'ha'), may hold values from -6 to 6
- w_first: bfloat16 [3, 3, 3, 4, 32], replicated, may hold values from -0.625 to 0.625
- w_second: bfloat16 [3, 3, 3, 32, 64], replicated, may hold values from -0.21875 to 0.21875
- w_third: bfloat16 [3, 3, 3, 64, 128], P(None, None, None, None, 'ha'), may hold values from -0.15625 to 0.15625
- cotangent: bfloat16 [128, 8, 8, 64], P('ha', 'dev'), may hold values from -6 to 6
Outputs:
- out_third: bfloat16 [128, 8, 8, 64], P('ha', 'dev')
- grad_first: float32 [3, 3, 3, 4, 32], replicated
- grad_second: float32 [3, 3, 3, 32, 64], replicated
- grad_third: float32 [3, 3, 3, 64, 128], P(None, None, None, None, 'ha')
The draws below stay inside these ranges and needn't reach their ends.
All inputs are finite; a program needn't handle non-finite values.
Results may differ from the reference program's by a relative error of at most 0.0063.
Values may be sent and summed in bfloat16 or wider, within the bound.
No kernel may reach another device: no remote copies, remote signals or barrier semaphores. Data moves between devices by JAX's collectives and lax.ppermute only.
A program may use at most 192 MiB of HBM per device.

```python
import jax
import jax.numpy as jnp
from jax import lax

CIN = 4
C1 = 32
C2 = 64
C3 = 128
W = 512
DEPTH = 64
HEIGHT = 64


def block_scale(stream_key, shape, pieces, least, high):
    def one(dim, blocks):
        steps = jax.random.uniform(jax.random.fold_in(jax.random.fold_in(stream_key, 6), dim), (blocks,), jnp.float32, least / len(pieces), high / len(pieces))
        return jnp.repeat(jnp.exp(steps), shape[dim] // blocks).reshape((-1,) + (1,) * (len(shape) - dim - 1))

    level = one(*pieces[0])
    for cut in pieces[1:]:
        level = level * one(*cut)
    return level


def noise(own_key, shape, deviation, bound, pieces=(), held_as=jnp.bfloat16):
    result = jax.random.normal(own_key, shape, jnp.float32) * deviation
    if len(pieces) > 0:
        result = block_scale(own_key, shape, pieces, -0.22, 0.18) * result
    return jnp.clip(result, min=-bound, max=bound).astype(held_as)


def setup_inputs(seed: int = 0) -> dict:
    key_of = jax.random.split(jax.random.key(seed), 6)
    volume = noise(key_of[0], (CIN, DEPTH, HEIGHT, W), 1.0, 6.0, ((1, 8), (2, 4)))
    w_first = noise(key_of[1], (3, 3, 3, CIN, C1), (27 * CIN) ** -0.5, 0.625)
    w_second = noise(key_of[2], (3, 3, 3, C1, C2), (27 * C1) ** -0.5, 0.21875)
    w_third = noise(key_of[3], (3, 3, 3, C2, C3), (27 * C2) ** -0.5, 0.15625, ((4, 4),))
    cotangent = noise(key_of[4], (C3, DEPTH // 8, HEIGHT // 8, W // 8), 1.0, 6.0, ((0, 4), (1, 8)))
    return {"volume": volume, "w_first": w_first, "w_second": w_second, "w_third": w_third, "cotangent": cotangent}


def convolve(inputs, kernel):
    return lax.conv_general_dilated(inputs[None], kernel, (2, 2, 2), [(1, 0)] * 3, dimension_numbers=('NCDHW', 'DHWIO', 'NCDHW'), preferred_element_type=jnp.float32)[0]

def exact_conv(inputs, kernel):
    return lax.conv_general_dilated(inputs[None], kernel, (2, 2, 2), [(1, 0)] * 3, dimension_numbers=('NCDHW', 'DHWIO', 'NCDHW'), precision=lax.Precision.HIGHEST)[0]

def leaky_relu(values):
    return 0.3 * values + 0.175 * jax.nn.softplus(4.0 * values)

def leaky_slope(values):
    return 0.3 + 0.7 * jax.nn.sigmoid(4.0 * values)

def kernel_grad(inputs, kernel, delta):
    inputs_full = inputs.astype(jnp.float32)

    def apply_kernel(weights):
        return exact_conv(inputs_full, weights)
    unused, pull = jax.vjp(apply_kernel, kernel.astype(jnp.float32))
    return pull(delta.astype(jnp.float32))[0]

def data_grad(inputs, kernel, delta):
    kernel_full = kernel.astype(jnp.float32)

    def apply_data(values):
        return exact_conv(values, kernel_full)
    unused, pull = jax.vjp(apply_data, inputs.astype(jnp.float32))
    return pull(delta.astype(jnp.float32))[0]

def cell_scale(array):
    return 1.0 / jnp.sqrt(jnp.float32(array.shape[1] * array.shape[2] * array.shape[3]))

def reference(volume, w_first, w_second, w_third, cotangent):
    pre_first = convolve(volume, w_first)
    act_first = leaky_relu(pre_first).astype(jnp.bfloat16)
    pre_second = convolve(act_first, w_second)
    act_second = leaky_relu(pre_second).astype(jnp.bfloat16)
    pre_third = convolve(act_second, w_third)
    out_third = leaky_relu(pre_third).astype(jnp.bfloat16)
    delta_third = (cotangent.astype(jnp.float32) * leaky_slope(pre_third)).astype(jnp.bfloat16)
    grad_third = kernel_grad(act_second, w_third, delta_third) * cell_scale(pre_third)
    back_second = data_grad(act_second, w_third, delta_third)
    delta_second = (back_second * leaky_slope(pre_second)).astype(jnp.bfloat16)
    grad_second = kernel_grad(act_first, w_second, delta_second) * cell_scale(pre_second)
    back_first = data_grad(act_first, w_second, delta_second)
    delta_first = (back_first * leaky_slope(pre_first)).astype(jnp.bfloat16)
    grad_first = kernel_grad(volume, w_first, delta_first) * cell_scale(pre_first)
    return (out_third, grad_first, grad_second, grad_third)
```

```python
import math

import jax
import jax.numpy as jnp
import numpy as np
from jax import lax
from jax.experimental import pallas as pl
from jax.experimental.pallas import tpu as pltpu
from jax.sharding import PartitionSpec as P

BF = jnp.bfloat16
F32 = jnp.float32
PARAMS = pltpu.CompilerParams(vmem_limit_bytes=48 * 1024 * 1024)


def shifted(block, axis, distance):
    devices = range(lax.axis_size(axis))
    route = [(i - distance, i) for i in devices if i - distance in devices]
    return lax.ppermute(block, axis, route)


def mm(left, right):
    return jnp.dot(left, right, preferred_element_type=F32)


def mm_nt(left, right):
    return lax.dot_general(left, right, (((1,), (1,)), ((), ())), preferred_element_type=F32)


def leaky_and_slope(z):
    u = 4.0 * z
    t = jnp.exp(-jnp.abs(u))
    s = 1.0 + t
    act = 0.3 * z + 0.175 * (jnp.maximum(u, 0.0) + jnp.log(s))
    r = 1.0 / s
    slope = 0.3 + 0.7 * jnp.where(u >= 0.0, r, t * r)
    return act, slope


def row_height(r):
    return np.where(r < 64, r % 16, (r - 64) % 8 - 8)


def row_channel(r):
    return np.where(r < 64, r // 16, (r - 64) // 8)


def constants(width):
    s = width // 8
    sel = np.zeros((width, 3 * 4 * s), np.float32)
    for e in range(3):
        for k, t in enumerate((0, 2, 1, 3)):
            for c in range(s):
                w = 8 * c + 2 * t - 1 + e
                if w >= 0:
                    sel[w, e * 4 * s + k * s + c] = 1
    cols = np.arange(288)
    a, r = cols // 96, cols % 96
    am = a * 4 + row_channel(r)
    h = row_height(r)
    rows = np.arange(352)
    j = rows // 32 - 3
    spread_o = (rows[:, None] % 32 == np.arange(32)[None]).astype(np.float32)
    spread_am = (np.arange(16)[:, None] == am[None]).astype(np.float32)
    mask = np.stack([(h[None] == (2 * j - 1 + b)[:, None]) for b in range(3)]).astype(np.float32)
    later = np.zeros((2 * s, 2 * s), np.float32)
    for c in range(s):
        later[c, s + c] = 1
        if c + 1 < s:
            later[s + c, c + 1] = 1
    pair = np.zeros((4 * s, 6 * s), np.float32)
    for k in range(2):
        for c in range(s):
            pair[k * 2 * s + c, 2 * s + k * s + c] = 1
            pair[k * 2 * s + s + c, 4 * s + k * s + c] = 1
            if c + 1 < s:
                pair[k * 2 * s + s + c, k * s + c + 1] = 1
    spread = np.zeros((2 * s, 12 * s), np.float32)
    for k in range(2):
        for c in range(s):
            base = k * 6 * s
            spread[k * s + c, base + c] = 1
            spread[k * s + c, base + 2 * s + s + c] = 1
            if c > 0:
                spread[k * s + c, base + 4 * s + s + c - 1] = 1
    return {
        "sel": sel, "spread_o": spread_o, "spread_am": spread_am, "mask": mask,
        "later": later, "pair": pair, "spread": spread,
    }


def prep_kernel(own_ref, sel_ref, wbe_ref, so_ref, sam_ref, mask_ref, x_ref, t_ref):
    x_ref[...] = mm(own_ref[...], sel_ref[...]).astype(BF)
    for e in range(3):
        total = None
        for b in range(3):
            rows = mm(so_ref[...], wbe_ref[b * 3 + e]).astype(BF)
            term = mm(rows, sam_ref[...]) * mask_ref[b].astype(F32)
            total = term if total is None else total + term
        t_ref[e] = total.astype(BF)


def forward_kernel(
    xown_ref, hz_ref, dd_ref, sel_ref, t_ref, w2t_ref, w3t_ref, cot_ref, later_ref, pair_ref,
    out_ref, d3_ref, g3_ref, sz_ref, sd_ref, x1_ref, a1_ref, slope1_ref, slope2_ref, a2_ref,
):
    low_dev = (lax.axis_index("dev") > 0).astype(F32)
    low_ha = (lax.axis_index("ha") > 0).astype(F32)
    x1_ref[0:672] = mm(dd_ref[...], sel_ref[...]).astype(BF)
    hz = mm(hz_ref[...], sel_ref[...]).astype(BF)
    for d in range(8):
        base = (7 + d) * 96
        x1_ref[base:base + 64] = xown_ref[d * 64:d * 64 + 64]
        x1_ref[base + 64:base + 96] = hz[d * 32:d * 32 + 32]
    for ii in range(7):
        lo = ii * 192
        z = None
        for e in range(3):
            term = mm(t_ref[e], x1_ref[lo:lo + 288, e * 256:e * 256 + 256])
            z = term if z is None else z + term
        act, slope = leaky_and_slope(z)
        rows = lax.broadcasted_iota(jnp.int32, act.shape, 0)
        keep = jnp.where(rows < 96, low_ha, 1.0)
        if ii < 3:
            keep = keep * low_dev
        act = (act * keep).astype(BF)
        a1_ref[ii, :, 128:384] = act
        a1_ref[ii, :, 0:128] = mm(act[:, 128:256], later_ref[...]).astype(BF)
        if ii >= 3:
            slope1_ref[ii - 3] = slope[96:352]

    def patch(p, q):
        return jnp.concatenate(
            [
                a1_ref[2 * p + 2 + a, (2 * q + 2 + b) * 32:(2 * q + 3 + b) * 32, e * 128:e * 128 + 128]
                for a in range(3) for b in range(3) for e in range(3)
            ], 0)

    w2t = w2t_ref[...]
    for p in range(-1, 2):
        for group in ((-1, 0), (1, 2), (3,)):
            x = jnp.concatenate([patch(p, q) for q in group], 1)
            act, slope = leaky_and_slope(mm(w2t, x))
            for k, q in enumerate(group):
                part = act[:, k * 128:k * 128 + 128]
                if p < 0:
                    part = part * low_dev
                if q < 0:
                    part = part * low_ha
                a2_ref[p + 1, (q + 1) * 64:(q + 2) * 64] = part.astype(BF)
                if p >= 0 and q >= 0:
                    slope2_ref[p, q * 64:q * 64 + 64] = slope[:, k * 128:k * 128 + 128]
    pieces = []
    for a in range(3):
        both = jnp.concatenate([a2_ref[a, 0:192], a2_ref[a, 128:320]], 1)
        spread = mm(both, pair_ref[...]).astype(BF)
        for b in range(3):
            for e in range(3):
                pieces.append(spread[b * 64:b * 64 + 64, e * 128:e * 128 + 128])
    x3 = jnp.concatenate(pieces, 0)
    act, slope = leaky_and_slope(mm(w3t_ref[...], x3))
    out_ref[...] = act.astype(BF)
    d3 = (cot_ref[...].astype(F32) * slope).astype(BF)
    d3_ref[...] = d3
    g3 = mm_nt(d3, x3).astype(BF)
    parts, _, lanes = g3_ref.shape
    for c in range(parts):
        have = min(max(1728 - c * lanes, 0), lanes)
        if have == lanes:
            g3_ref[c] = g3[:, c * lanes:(c + 1) * lanes]
        else:
            g3_ref[c] = jnp.zeros((128, lanes), BF)
            if have > 0:
                g3_ref[c, :, 0:have] = g3[:, c * lanes:c * lanes + have]
    sz_ref[0:128] = d3
    sd_ref[0:128] = d3
    for p in range(2):
        sz_ref[128 + 64 * p:192 + 64 * p] = slope2_ref[p, 0:64].astype(BF)
    sd_ref[128:384] = slope2_ref[0].astype(BF)


def backward_kernel(
    d3_ref, rz_ref, rd_ref, x1_ref, a1_ref, slope1_ref, slope2_ref, w3g_ref, w2e_ref, w2o_ref,
    later_ref, spread_ref, so_ref, sam_ref, mask_ref,
    msg_ref, d2_ref, d1_ref,
):
    spread = spread_ref[...]

    def blocks(pair, last):
        both = mm(pair, spread).astype(BF)
        lone = mm(last, spread[:, 0:384]).astype(BF)
        cols = [both[:, 0:384], both[:, 384:768], lone]
        return jnp.concatenate(
            [jnp.concatenate([c[:, e * 128:e * 128 + 128] for e in range(3)], 0) for c in cols], 1)

    u0 = mm(w3g_ref[192:576], blocks(d3_ref[...], rz_ref[0:128]))
    u1 = mm(w3g_ref[0:384], blocks(rd_ref[0:128], rd_ref[384:512]))
    u = {(0, 1): u0[0:192], (0, 2): u0[192:384], (1, 0): u1[0:192], (1, 1): u1[192:384]}
    taps = {0: ((1, 0),), 1: ((2, 0), (0, 1)), 2: ((1, 1),), 3: ((2, 1), (0, 2)), 4: ((1, 2),)}
    for x in range(3):
        for y in range(5):
            back = None
            for a, i in taps[x]:
                for b, j in taps[y]:
                    term = u[(i, a)][b * 64:b * 64 + 64, j * 128:j * 128 + 128]
                    back = term if back is None else back + term
            if x < 2 and y < 4:
                slope = slope2_ref[x, y * 64:y * 64 + 64]
            elif x < 2:
                slope = rz_ref[128 + 64 * x:192 + 64 * x].astype(F32)
            elif y < 4:
                slope = rd_ref[128 + 64 * y:192 + 64 * y].astype(F32)
            else:
                slope = rd_ref[512:576].astype(F32)
            d2_ref[x, :, y * 128:y * 128 + 128] = (back * slope).astype(BF)

    def patch(p, q):
        return jnp.concatenate(
            [
                a1_ref[2 * p + 2 + a, (2 * q + 2 + b) * 32:(2 * q + 3 + b) * 32, e * 128:e * 128 + 128]
                for a in range(3) for b in range(3) for e in range(3)
            ], 0)

    g2 = None
    for p in range(2):
        for q in (0, 2):
            x = jnp.concatenate([patch(p, q), patch(p, q + 1)], 1)
            term = mm_nt(x, d2_ref[p, :, q * 128:q * 128 + 256])
            g2 = term if g2 is None else g2 + term
    msg_ref[0:432] = jnp.concatenate([g2[0:432], g2[432:864]], 1).astype(BF)

    ue, uo = {}, {}
    for p, first, end in ((0, 1, 3), (1, 0, 3), (2, 0, 1)):
        d2 = d2_ref[p]
        moved = jnp.concatenate(
            [mm_nt(d2[:, q * 128:q * 128 + 128], later_ref[...]).astype(BF) for q in range(5)], 1)
        e_part = mm(w2e_ref[first * 96:end * 96], d2)
        o_part = mm(w2o_ref[first * 96:end * 96], jnp.concatenate([d2, moved], 0))
        for a in range(first, end):
            lo = (a - first) * 96
            ue[(p, a)] = e_part[lo:lo + 96]
            uo[(p, a)] = o_part[lo:lo + 96]
    for x in range(4):
        for y in range(8):
            if y % 2 == 0:
                y_taps = ((1, y // 2),)
            else:
                y_taps = ((2, y // 2), (0, y // 2 + 1))
            x_taps = ((1, x // 2),) if x % 2 == 0 else ((2, x // 2), (0, x // 2 + 1))
            for k, source in ((0, ue), (1, uo)):
                back = None
                for a, p in x_taps:
                    for b, q in y_taps:
                        term = source[(p, a)][b * 32:b * 32 + 32, q * 128:q * 128 + 128]
                        back = term if back is None else back + term
                slope = slope1_ref[x, y * 32:y * 32 + 32, k * 128:k * 128 + 128]
                d1_ref[y * 32:y * 32 + 32, x * 256 + k * 128:x * 256 + k * 128 + 128] = (back * slope).astype(BF)

    d1 = d1_ref[...]
    so = so_ref[0:256]
    sam = sam_ref[...]
    columns = []
    grads = []
    for e in range(3):
        x = jnp.concatenate([x1_ref[(2 * i + 6) * 96:(2 * i + 6) * 96 + 288, e * 256:e * 256 + 256] for i in range(4)], 1)
        grads.append(mm_nt(x, d1))
    for b in range(3):
        for e in range(3):
            kept = grads[e] * mask_ref[b].astype(F32)
            high = kept.astype(BF)
            low = (kept - high.astype(F32)).astype(BF)
            columns.append(mm(high, so) + mm(low, so))
    wide = jnp.concatenate(columns, 1)
    high = wide.astype(BF)
    low = (wide - high.astype(F32)).astype(BF)
    g1 = (mm(sam, high) + mm(sam, low)).astype(BF)
    msg_ref[432:512] = jnp.zeros((80, 128), BF)
    msg_ref[432:448] = g1[:, 0:128]
    msg_ref[448:464] = g1[:, 128:256]
    msg_ref[464:480, 0:32] = g1[:, 256:288]


def local(volume, w_first, w_second, w_third, cotangent):
    nd, nh = lax.axis_size("dev"), lax.axis_size("ha")
    depth_total = volume.shape[1] * nd
    height_total = volume.shape[2] * nh
    width = volume.shape[3]
    cells = depth_total * height_total * width
    scale_first, scale_second, scale_third = (1.0 / math.sqrt(cells // 8 ** k) for k in (1, 2, 3))
    const = {k: jnp.asarray(v, BF) for k, v in constants(width).items()}
    vmem = pltpu.VMEM

    hz = shifted(volume[:, :, 8:].transpose(1, 0, 2, 3).reshape(8, 32, width), "ha", 1)
    own = volume.transpose(1, 0, 2, 3).reshape(8, 64, width)
    dd = shifted(jnp.concatenate([own[1:], hz[1:]], 1), "dev", 1)

    w3t = lax.all_gather(w_third.reshape(1728, -1).T, "ha", axis=0, tiled=True)
    share = cotangent[:, 0].reshape(-1, nh, 2, 64).transpose(1, 0, 2, 3)
    cot = lax.all_to_all(share, "ha", 0, 0, tiled=True)
    cot = cot.reshape(128, 128)
    w2t = w_second.reshape(864, 64).T
    wbe = w_first.transpose(1, 2, 4, 0, 3).reshape(9, 32, 12)
    wbe = jnp.pad(wbe, ((0, 0), (0, 0), (0, 4)))

    xown, t1 = pl.pallas_call(
        prep_kernel,
        out_shape=(jax.ShapeDtypeStruct((512, 768), BF), jax.ShapeDtypeStruct((3, 352, 288), BF)),
        compiler_params=PARAMS,
        cost_estimate=pl.CostEstimate(flops=1 << 29, bytes_accessed=1 << 22, transcendentals=0),
        name="prep",
    )(own.reshape(512, width), const["sel"], wbe, const["spread_o"], const["spread_am"], const["mask"])

    out3, d3, g3, sz, sd, x1, a1, slope1, slope2 = pl.pallas_call(
        forward_kernel,
        out_shape=(
            jax.ShapeDtypeStruct((128, 128), BF),
            jax.ShapeDtypeStruct((128, 128), BF),
            jax.ShapeDtypeStruct((nd, 128, 2048 // nd), BF),
            jax.ShapeDtypeStruct((256, 128), BF),
            jax.ShapeDtypeStruct((384, 128), BF),
            jax.ShapeDtypeStruct((1440, 768), BF),
            jax.ShapeDtypeStruct((7, 352, 384), BF),
            jax.ShapeDtypeStruct((4, 256, 256), F32),
            jax.ShapeDtypeStruct((2, 256, 128), F32),
        ),
        scratch_shapes=[vmem((3, 320, 128), BF)],
        compiler_params=PARAMS,
        cost_estimate=pl.CostEstimate(flops=1 << 32, bytes_accessed=1 << 23, transcendentals=1 << 21),
        name="forward",
    )(xown, hz.reshape(256, width), dd.reshape(672, width), const["sel"], t1, w2t, w3t, cot, const["later"], const["pair"])

    rz = shifted(sz, "ha", -1)
    rd = shifted(jnp.concatenate([sd, rz[0:192]], 0), "dev", -1)

    sent = g3.reshape(nd * nh, 128 // nh, 2048 // nd)
    parts = lax.all_to_all(sent, ("dev", "ha"), 0, 0, tiled=True)
    chunk = jnp.sum(parts.astype(F32), 0) * scale_third
    everything = lax.all_gather(chunk, "dev", axis=0)
    grad_third = everything.transpose(1, 0, 2).reshape(128 // nh, 2048)[:, :1728]
    grad_third = grad_third.T.reshape(3, 3, 3, 64, 128 // nh)
    share = lax.all_to_all(out3.reshape(nh, 128 // nh, 128), "ha", 0, 0, tiled=True)
    out_third = share.reshape(nh, 128 // nh, 2, 64).transpose(1, 0, 2, 3).reshape(128 // nh, 1, 2 * nh, 64)

    order = jnp.array([1, 2, 0])
    w3g = w3t.reshape(128, 9, 3, 64).transpose(1, 3, 2, 0)
    w3g = jnp.concatenate([w3g[:, :, 1], w3g[:, :, 2], w3g[:, :, 0]], 2).reshape(576, 384)
    taps = w_second.reshape(9, 3, 32, 64)
    w2e = taps[:, 1].reshape(288, 64)
    w2o = jnp.concatenate([taps[:, 2], taps[:, 0]], 2).reshape(288, 128)
    mask_own = const["mask"][:, 96:].transpose(0, 2, 1)
    msg = pl.pallas_call(
        backward_kernel,
        out_shape=jax.ShapeDtypeStruct((512, 128), BF),
        scratch_shapes=[vmem((3, 64, 640), BF), vmem((256, 1024), BF)],
        compiler_params=PARAMS,
        cost_estimate=pl.CostEstimate(flops=1 << 32, bytes_accessed=1 << 23, transcendentals=0),
        name="backward",
    )(d3, rz, rd, x1, a1, slope1, slope2, w3g, w2e, w2o, const["later"], const["spread"],
      const["spread_o"], const["spread_am"], mask_own)

    n = nd * nh
    parts = lax.all_to_all(msg.reshape(n, 512 // n, 128), ("dev", "ha"), 0, 0, tiled=True)
    chunk = jnp.sum(parts.astype(F32), 0).astype(BF)
    spread = jnp.broadcast_to(chunk[None], (n, 512 // n, 128))
    total = lax.all_to_all(spread, ("dev", "ha"), 0, 0, tiled=True).reshape(512, 128).astype(F32)
    grad_second = jnp.concatenate([total[0:432, 0:64], total[0:432, 64:128]], 0) * scale_second
    grad_second = grad_second.reshape(3, 3, 3, 32, 64)
    flat = jnp.concatenate([total[432:444], total[448:460], total[464:476, 0:32]], 1) * scale_first
    grad_first = flat.reshape(3, 4, 3, 3, 32).transpose(0, 2, 3, 1, 4)
    return out_third, grad_first, grad_second, grad_third


def solution(mesh):
    placed = (
        P(None, "dev", "ha", None),
        P(),
        P(),
        P(None, None, None, None, "ha"),
        P("ha", "dev", None, None),
    )
    return jax.shard_map(
        local,
        mesh=mesh,
        in_specs=placed,
        out_specs=(P("ha", "dev", None, None), P(), P(), P(None, None, None, None, "ha")),
        check_vma=False,
    )
```

```python
import functools
import math

import jax
import jax.numpy as jnp
import numpy as np
from jax import lax
from jax.experimental import pallas as pl
from jax.experimental.pallas import tpu as pltpu
from jax.sharding import PartitionSpec as P

BF = jnp.bfloat16
F32 = jnp.float32
PARK = {"x1": (0, 2592), "a1": (2592, 1760), "x3": (4352, 1728), "slope1": (0, 1024), "slope2": (1024, 512)}
PARK_SHAPES = ((90112, 384), (67584, 256))


def parked(park, name, lanes):
    first, count = PARK[name]
    return park.at[first:first + count, 0:lanes]


def call(name, body, inputs, far_inputs, outputs, far_outputs=(), scratch=(), limit=24, flops=1 << 28):
    near, far = pl.BlockSpec(memory_space=pltpu.VMEM), pl.BlockSpec(memory_space=pl.ANY)
    return pl.pallas_call(
        body,
        out_shape=(*outputs, *far_outputs),
        in_specs=[near] * len(inputs) + [far] * len(far_inputs),
        out_specs=(near,) * len(outputs) + (far,) * len(far_outputs),
        scratch_shapes=list(scratch),
        compiler_params=pltpu.CompilerParams(vmem_limit_bytes=limit * 1024 * 1024),
        cost_estimate=pl.CostEstimate(flops=flops, bytes_accessed=1 << 20, transcendentals=0),
        name=name,
    )(*inputs, *far_inputs)


def array(dtype, *shape):
    return jax.ShapeDtypeStruct(shape, dtype)


def shifted(block, axis, distance):
    devices = range(lax.axis_size(axis))
    route = [(i - distance, i) for i in devices if i - distance in devices]
    return lax.ppermute(block, axis, route)


def diagonal(block):
    nd, nh = lax.axis_size("dev"), lax.axis_size("ha")
    route = [(i * nh + j, (i + 1) * nh + j + 1) for i in range(nd - 1) for j in range(nh - 1)]
    return lax.ppermute(block, ("dev", "ha"), route)


def mm(left, right):
    return jnp.dot(left, right, preferred_element_type=F32)


def mm_nt(left, right):
    return lax.dot_general(left, right, (((1,), (1,)), ((), ())), preferred_element_type=F32)


def leaky_and_slope(z):
    u = 4.0 * z
    t = jnp.exp(-jnp.abs(u))
    s = 1.0 + t
    act = 0.3 * z + 0.175 * (jnp.maximum(u, 0.0) + jnp.log(s))
    r = 1.0 / s
    slope = 0.3 + 0.7 * jnp.where(u >= 0.0, r, t * r)
    return act, slope


def row_height(r):
    return np.where(r < 64, r % 16, (r - 64) % 8 - 8)


def row_channel(r):
    return np.where(r < 64, r // 16, (r - 64) // 8)


def constants(width):
    s = width // 8
    sel = np.zeros((width, 3 * 4 * s), np.float32)
    for e in range(3):
        for k, t in enumerate((0, 2, 1, 3)):
            for c in range(s):
                w = 8 * c + 2 * t - 1 + e
                if w >= 0:
                    sel[w, e * 4 * s + k * s + c] = 1
    r = np.arange(96)
    hot = np.zeros((11, 48, 288), np.float32)
    for j in range(11):
        for a in range(3):
            for b in range(3):
                for k in range(96):
                    if row_height(k) == 2 * (j - 3) - 1 + b:
                        hot[j, (a * 4 + row_channel(k)) * 3 + b, a * 96 + k] = 1
    cols = np.arange(288)
    a, r = cols // 96, cols % 96
    am = a * 4 + row_channel(r)
    j = np.arange(256) // 32
    spread_o = (np.arange(256)[:, None] % 32 == np.arange(32)[None]).astype(np.float32)
    spread_am = (np.arange(16)[:, None] == am[None]).astype(np.float32)
    mask = np.stack([(row_height(r)[:, None] == (2 * j - 1 + b)[None]) for b in range(3)]).astype(np.float32)
    later = np.zeros((2 * s, 2 * s), np.float32)
    for c in range(s):
        later[c, s + c] = 1
        if c + 1 < s:
            later[s + c, c + 1] = 1
    pair = np.zeros((4 * s, 6 * s), np.float32)
    for k in range(2):
        for c in range(s):
            pair[k * 2 * s + c, 2 * s + k * s + c] = 1
            pair[k * 2 * s + s + c, 4 * s + k * s + c] = 1
            if c + 1 < s:
                pair[k * 2 * s + s + c, k * s + c + 1] = 1
    spread = np.zeros((2 * s, 12 * s), np.float32)
    for k in range(2):
        for c in range(s):
            base = k * 6 * s
            spread[k * s + c, base + c] = 1
            spread[k * s + c, base + 2 * s + s + c] = 1
            if c > 0:
                spread[k * s + c, base + 4 * s + s + c - 1] = 1
    return {
        "sel": sel, "hot": hot, "spread_o": spread_o, "spread_am": spread_am, "mask": mask,
        "later": later, "pair": pair, "spread": spread,
    }


def first_body(
    wt_ref, later_ref, w2_ref, pair_ref, *refs,
):
    sources, refs = refs[:6], refs[6:]
    park_b, park_f = refs[:2]
    held, refs = refs[2:8], refs[8:]
    hot_ref, sel_ref, volume_ref, dd_ref, dz_ref, hz_ref = held
    (x1_ref, a1_ref, t_ref, a2_ref, x1_out, a1_out, slope1_ref, slope2_ref, x3_ref, sems, came) = refs
    fetches = [pltpu.make_async_copy(sources[i], held[i], came.at[i]) for i in range(6)]
    for fetch in fetches:
        fetch.start()
    sends = []

    def send(source, park, name):
        copy = pltpu.make_async_copy(source, parked(park, name, source.shape[1]), sems.at[len(sends)])
        copy.start()
        sends.append(copy)

    low_dev = (lax.axis_index("dev") > 0).astype(F32)
    low_ha = (lax.axis_index("ha") > 0).astype(F32)
    wt = wt_ref[...]
    fetches[0].wait()
    for j in range(11):
        part = mm(wt, hot_ref[j])
        t_ref[j * 32:j * 32 + 32] = jnp.concatenate([part[0:32], part[32:64], part[64:96]], 1).astype(BF)
    fetches[1].wait()
    sel = sel_ref[...]
    for volume, edges, first, skip, given in ((volume_ref, hz_ref, 7, 0, (2, 5)), (dd_ref, dz_ref, -1, 1, (3, 4))):
        for i in given:
            fetches[i].wait()
        side = mm(edges[...].reshape(256, -1), sel).astype(BF)
        main = [mm(volume[m, skip:].reshape((8 - skip) * 16, -1), sel).astype(BF) for m in range(4)]
        for d in range(skip, 8):
            base = (first + d) * 96
            for e in range(3):
                lanes = slice(e * 256, e * 256 + 256)
                for m in range(4):
                    x1_ref[e, base + m * 16:base + m * 16 + 16] = main[m][(d - skip) * 16:(d - skip) * 16 + 16, lanes]
                x1_ref[e, base + 64:base + 96] = side[d * 32:d * 32 + 32, lanes]
    for e in range(3):
        x1_out[e * 864:e * 864 + 864] = x1_ref[e, 576:1440]
    send(x1_out, park_b, "x1")
    t = t_ref[...]
    later = later_ref[...]
    for ii in range(7):
        lo = ii * 192
        z = mm(t, jnp.concatenate([x1_ref[e, lo:lo + 288] for e in range(3)], 0))
        act, slope = leaky_and_slope(z)
        rows = lax.broadcasted_iota(jnp.int32, act.shape, 0)
        keep = jnp.where(rows < 96, low_ha, 1.0)
        if ii < 3:
            keep = keep * low_dev
        act = (act * keep).astype(BF)
        a1_ref[ii, :, 128:384] = act
        a1_ref[ii, :, 0:128] = mm(act[:, 128:256], later).astype(BF)
        if ii >= 2:
            a1_out[(ii - 2) * 352:(ii - 1) * 352] = a1_ref[ii]
        if ii >= 3:
            slope1_ref[(ii - 3) * 256:(ii - 2) * 256] = slope[96:352]
    send(a1_out, park_b, "a1")
    send(slope1_ref, park_f, "slope1")

    def patch(p, q):
        return jnp.concatenate(
            [
                a1_ref[2 * p + 2 + a, (2 * q + 2 + b) * 32:(2 * q + 3 + b) * 32, e * 128:e * 128 + 128]
                for a in range(3) for b in range(3) for e in range(3)
            ], 0)

    w2t = w2_ref[...].astype(F32).T.astype(BF)
    for p in range(-1, 2):
        for group in ((-1, 0), (1, 2), (3,)):
            x = jnp.concatenate([patch(p, q) for q in group], 1)
            act, slope = leaky_and_slope(mm(w2t, x))
            for k, q in enumerate(group):
                part = act[:, k * 128:k * 128 + 128]
                if p < 0:
                    part = part * low_dev
                if q < 0:
                    part = part * low_ha
                a2_ref[p + 1, (q + 1) * 64:(q + 2) * 64] = part.astype(BF)
                if p >= 0 and q >= 0:
                    slope2_ref[p * 256 + q * 64:p * 256 + q * 64 + 64] = slope[:, k * 128:k * 128 + 128]
    send(slope2_ref, park_f, "slope2")
    for a in range(3):
        both = jnp.concatenate([a2_ref[a, 0:192], a2_ref[a, 128:320]], 1)
        spread = mm(both, pair_ref[...]).astype(BF)
        for b in range(3):
            for e in range(3):
                at = ((a * 3 + b) * 3 + e) * 64
                x3_ref[at:at + 64] = spread[b * 64:b * 64 + 64, e * 128:e * 128 + 128]
    send(x3_ref, park_b, "x3")
    for copy in sends:
        copy.wait()


def third_body(both_ref, order_ref, park_b, park_f, out_ref, d3_ref, g3_ref, sz_ref, sd_ref, x3_ref, slope2_ref, sems):
    fetches = (
        pltpu.make_async_copy(parked(park_b, "x3", 128), x3_ref, sems.at[0]),
        pltpu.make_async_copy(parked(park_f, "slope2", 128), slope2_ref, sems.at[1]),
    )
    for fetch in fetches:
        fetch.start()
    for fetch in fetches:
        fetch.wait()
    x3 = x3_ref[...]
    act, slope = leaky_and_slope(mm(both_ref[:, 128:1856], x3))
    out_ref[...] = act.astype(BF)
    d3 = (both_ref[:, 0:128].astype(F32) * slope).astype(BF)
    d3_ref[...] = d3
    sz_ref[0:128] = d3
    sd_ref[0:128] = d3
    for p in range(2):
        sz_ref[128 + 64 * p:192 + 64 * p] = slope2_ref[256 * p:256 * p + 64].astype(BF)
    sd_ref[128:384] = slope2_ref[0:256].astype(BF)
    ordered = mm(order_ref[...], d3).astype(BF)
    wide = jnp.concatenate([x3, jnp.zeros((64, 128), BF)], 0)
    g3 = mm_nt(ordered, wide).astype(BF)
    for k in range(14):
        g3_ref[k] = g3[:, k * 128:k * 128 + 128]
    g3_ref[14:16] = jnp.zeros((2, 128, 128), BF)


def sum_body(g3_ref, msg_ref, out_ref):
    nd, nh = out_ref.shape[0], out_ref.shape[1]
    g3 = jnp.sum(g3_ref[...].astype(F32), 0)
    msg = jnp.sum(msg_ref[...].astype(F32), 0)
    rows = g3.shape[0] // nh
    for h in range(nh):
        block = jnp.concatenate([g3[h * rows:(h + 1) * rows], msg], 0).astype(BF)
        for d in range(nd):
            out_ref[d, h] = block


def unpack_body(scales, total_ref, g1_ref, g2_ref, g3_ref):
    n, both, _ = total_ref.shape
    lot = 512 // n
    rows = both - lot
    slices = n // 16
    for tap in range(27):
        for s in range(slices):
            part = total_ref[tap // 2 * slices + s, 0:rows, tap % 2 * 64:tap % 2 * 64 + 64]
            g3_ref[tap, s * rows:(s + 1) * rows] = part.astype(F32) * scales[2]
    for k in range(2):
        part = total_ref[0:g2_ref.shape[1], rows:, k * 64:k * 64 + 64]
        g2_ref[k] = part.astype(F32) * scales[1]
    for block in range(3):
        lots = [total_ref[(432 + block * 16) // lot + i, rows:].astype(F32) for i in range(16 // lot)]
        part = jnp.concatenate(lots, 0) * scales[0]
        for k in range(4 if block < 2 else 1):
            for a in range(3):
                g1_ref[a * 9 + block * 4 + k] = part[a * 4:a * 4 + 4, k * 32:k * 32 + 32]


def backward_body(
    spread_ref, d3_ref, rz_ref, rd_ref, w3g_ref, w2_ref, later_ref, so_ref, sam_ref, mask_ref,
    park_b, park_f,
    msg_ref, d2_ref, d1_ref, slope2_ref, a1_ref, slope1_ref, x1_ref, sems,
):
    fetches = {}
    for i, (park, name, target) in enumerate(
            ((park_f, "slope2", slope2_ref), (park_b, "a1", a1_ref), (park_f, "slope1", slope1_ref), (park_b, "x1", x1_ref))):
        fetches[name] = pltpu.make_async_copy(parked(park, name, target.shape[1]), target, sems.at[i])
        fetches[name].start()
    spread = spread_ref[...]

    def blocks(pair, last):
        both = mm(pair, spread).astype(BF)
        lone = mm(last, spread[:, 0:384]).astype(BF)
        cols = [both[:, 0:384], both[:, 384:768], lone]
        return jnp.concatenate(
            [jnp.concatenate([c[:, e * 128:e * 128 + 128] for e in range(3)], 0) for c in cols], 1)

    u0 = mm(w3g_ref[192:576], blocks(d3_ref[...], rz_ref[0:128]))
    u1 = mm(w3g_ref[0:384], blocks(rd_ref[0:128], rd_ref[384:512]))
    u = {(0, 1): u0[0:192], (0, 2): u0[192:384], (1, 0): u1[0:192], (1, 1): u1[192:384]}
    fetches["slope2"].wait()
    taps = {0: ((1, 0),), 1: ((2, 0), (0, 1)), 2: ((1, 1),), 3: ((2, 1), (0, 2)), 4: ((1, 2),)}
    for x in range(3):
        for y in range(5):
            back = None
            for a, i in taps[x]:
                for b, j in taps[y]:
                    term = u[(i, a)][b * 64:b * 64 + 64, j * 128:j * 128 + 128]
                    back = term if back is None else back + term
            if x < 2 and y < 4:
                slope = slope2_ref[x * 256 + y * 64:x * 256 + y * 64 + 64]
            elif x < 2:
                slope = rz_ref[128 + 64 * x:192 + 64 * x].astype(F32)
            elif y < 4:
                slope = rd_ref[128 + 64 * y:192 + 64 * y].astype(F32)
            else:
                slope = rd_ref[512:576].astype(F32)
            d2_ref[x, :, y * 128:y * 128 + 128] = (back * slope).astype(BF)

    def at(p, a, q, b):
        return (2 * p + a) * 352 + (2 * q + b) * 32

    def patch(p, q):
        return jnp.concatenate(
            [
                a1_ref[at(p, a, q + 1, b):at(p, a, q + 1, b) + 32, e * 128:e * 128 + 128]
                for a in range(3) for b in range(3) for e in range(3)
            ], 0)

    fetches["a1"].wait()
    g2 = None
    for p in range(2):
        for q in (0, 2):
            x = jnp.concatenate([patch(p, q), patch(p, q + 1)], 1)
            term = mm_nt(x, d2_ref[p, :, q * 128:q * 128 + 256])
            g2 = term if g2 is None else g2 + term
    msg_ref[0:432] = jnp.concatenate([g2[0:432], g2[432:864]], 1).astype(BF)

    taps = w2_ref[...].reshape(9, 3, 32, 64)
    w2e = taps[:, 1].reshape(288, 64)
    w2o = jnp.concatenate([taps[:, 2].reshape(288, 64), taps[:, 0].reshape(288, 64)], 1)
    later = later_ref[...]
    ue, uo = {}, {}
    for p, first, end in ((0, 1, 3), (1, 0, 3), (2, 0, 1)):
        d2 = d2_ref[p]
        moved = jnp.concatenate(
            [mm_nt(d2[:, q * 128:q * 128 + 128], later).astype(BF) for q in range(5)], 1)
        e_part = mm(w2e[first * 96:end * 96], d2)
        o_part = mm(w2o[first * 96:end * 96], jnp.concatenate([d2, moved], 0))
        for a in range(first, end):
            lo = (a - first) * 96
            ue[(p, a)] = e_part[lo:lo + 96]
            uo[(p, a)] = o_part[lo:lo + 96]
    fetches["slope1"].wait()
    for x in range(4):
        for y in range(8):
            if y % 2 == 0:
                y_taps = ((1, y // 2),)
            else:
                y_taps = ((2, y // 2), (0, y // 2 + 1))
            x_taps = ((1, x // 2),) if x % 2 == 0 else ((2, x // 2), (0, x // 2 + 1))
            for k, source in ((0, ue), (1, uo)):
                back = None
                for a, p in x_taps:
                    for b, q in y_taps:
                        term = source[(p, a)][b * 32:b * 32 + 32, q * 128:q * 128 + 128]
                        back = term if back is None else back + term
                slope = slope1_ref[x * 256 + y * 32:x * 256 + y * 32 + 32, k * 128:k * 128 + 128]
                d1_ref[y * 32:y * 32 + 32, x * 256 + k * 128:x * 256 + k * 128 + 128] = (back * slope).astype(BF)

    d1 = d1_ref[...]
    so = so_ref[...]
    sam = sam_ref[...]
    columns = []
    fetches["x1"].wait()
    x = jnp.concatenate(
        [jnp.concatenate([x1_ref[e * 864 + i * 192:e * 864 + i * 192 + 288] for e in range(3)], 0) for i in range(4)], 1)
    wide = mm_nt(x, d1)
    grads = [wide[e * 288:e * 288 + 288] for e in range(3)]
    for b in range(3):
        for e in range(3):
            kept = grads[e] * mask_ref[b].astype(F32)
            high = kept.astype(BF)
            low = (kept - high.astype(F32)).astype(BF)
            columns.append(mm(high, so) + mm(low, so))
    wide = jnp.concatenate(columns, 1)
    high = wide.astype(BF)
    low = (wide - high.astype(F32)).astype(BF)
    g1 = (mm(sam, high) + mm(sam, low)).astype(BF)
    msg_ref[432:512] = jnp.zeros((80, 128), BF)
    msg_ref[432:448] = g1[:, 0:128]
    msg_ref[448:464] = g1[:, 128:256]
    msg_ref[464:480, 0:32] = g1[:, 256:288]


def local(volume, w_first, w_second, w_third, cotangent):
    nd, nh = lax.axis_size("dev"), lax.axis_size("ha")
    depth_total = volume.shape[1] * nd
    height_total = volume.shape[2] * nh
    width = volume.shape[3]
    cells = depth_total * height_total * width
    scale_first, scale_second, scale_third = (1.0 / math.sqrt(cells // 8 ** k) for k in (1, 2, 3))
    const = {k: jnp.asarray(v, BF) for k, v in constants(width).items()}
    vmem = pltpu.VMEM

    edge = volume[:, :, 8:].transpose(1, 0, 2, 3).reshape(8, 32, width)
    dd = shifted(volume, "dev", 1)
    dz = diagonal(edge)
    hz = shifted(edge, "ha", 1)

    share = cotangent[:, 0].reshape(-1, nh, 2, 64).transpose(1, 0, 2, 3).reshape(nh, -1, 128)
    piece = w_third.reshape(1728, -1).T
    both = jnp.concatenate([share, jnp.broadcast_to(piece[None], (nh,) + piece.shape)], 2)
    both = lax.all_to_all(both, "ha", 0, 0, tiled=True).reshape(128, 1856)
    wt = w_first.transpose(2, 4, 0, 3, 1).reshape(96, 36)
    wt = jnp.pad(wt, ((0, 0), (0, 12)))
    w2 = w_second.reshape(864, 64)
    dma = pltpu.SemaphoreType.DMA
    borrowed = [const["hot"], const["sel"], volume, dd, dz, hz]
    park_b, park_f = call(
        "first", first_body,
        [wt, const["later"], w2, const["pair"]], borrowed, [],
        [array(BF, *PARK_SHAPES[0]), array(F32, *PARK_SHAPES[1])],
        [*(vmem(x.shape, BF) for x in borrowed),
         vmem((3, 1440, 256), BF), vmem((7, 352, 384), BF), vmem((352, 864), BF), vmem((3, 320, 128), BF),
         vmem((2592, 256), BF), vmem((1760, 384), BF), vmem((1024, 256), F32), vmem((512, 128), F32),
         vmem((1728, 128), BF), dma((5,)), dma((6,))],
        63, 1 << 33)

    n = nd * nh
    slices = n // 16
    order = np.arange(128).reshape(nh, slices, -1).transpose(1, 0, 2).reshape(-1)
    order = jnp.asarray(np.eye(128)[order], BF)
    out3, d3, g3, sz, sd = call(
        "third", third_body, [both, order], [park_b, park_f],
        [array(BF, 128, 128), array(BF, 128, 128), array(BF, 16, 128, 128), array(BF, 256, 128), array(BF, 384, 128)],
        (), [vmem((1728, 128), BF), vmem((512, 128), F32), dma((2,))], 8)

    g3_parts = lax.all_to_all(g3.reshape(n, 2048 // n, 128), ("dev", "ha"), 0, 0, tiled=True)
    rz = shifted(sz, "ha", -1)
    rd = shifted(jnp.concatenate([sd, rz[0:192]], 0), "dev", -1)

    share = lax.all_to_all(out3.reshape(nh, 128 // nh, 128), "ha", 0, 0, tiled=True)
    out_third = share.reshape(nh, 128 // nh, 2, 64).transpose(1, 0, 2, 3).reshape(128 // nh, 1, 2 * nh, 64)

    w3g = both[:, 128:].reshape(128, 9, 3, 64).transpose(1, 3, 2, 0)
    w3g = jnp.concatenate([w3g[:, :, 1], w3g[:, :, 2], w3g[:, :, 0]], 2).reshape(576, 384)
    msg, = call(
        "backward", backward_body,
        [const["spread"], d3, rz, rd, w3g, w2, const["later"], const["spread_o"], const["spread_am"], const["mask"]],
        [park_b, park_f], [array(BF, 512, 128)], (),
        [vmem((3, 64, 640), BF), vmem((256, 1024), BF), vmem((512, 128), F32), vmem((1760, 384), BF),
         vmem((1024, 256), F32), vmem((2592, 256), BF), dma((4,))],
        24, 1 << 36)

    g3_parts, msg = lax.optimization_barrier((g3_parts, msg))
    msg_parts = lax.all_to_all(msg.reshape(n, 512 // n, 128), ("dev", "ha"), 0, 0, tiled=True)
    rows = 2048 // n // nh
    slices, = call("sum", sum_body, [g3_parts, msg_parts], [], [array(BF, nd, nh, rows + 512 // n, 128)], limit=8)
    total = lax.all_to_all(slices.reshape(n, rows + 512 // n, 128), ("dev", "ha"), 0, 0, tiled=True)
    scales = (scale_first, scale_second, scale_third)
    g1, g2, g3 = call(
        "unpack", functools.partial(unpack_body, scales), [total], [],
        [array(F32, 27, 4, 32), array(F32, 2, 432 * n // 512, 512 // n, 64), array(F32, 27, 128 // nh, 64)], limit=8)
    grad_first = g1.reshape(3, 3, 3, 4, 32)
    grad_second = g2.reshape(3, 3, 3, 32, 64)
    grad_third = g3.transpose(0, 2, 1).reshape(3, 3, 3, 64, 128 // nh)
    return out_third, grad_first, grad_second, grad_third


def solution(mesh):
    placed = (
        P(None, "dev", "ha", None),
        P(),
        P(),
        P(None, None, None, None, "ha"),
        P("ha", "dev", None, None),
    )
    return jax.shard_map(
        local,
        mesh=mesh,
        in_specs=placed,
        out_specs=(P("ha", "dev", None, None), P(), P(), P(None, None, None, None, "ha")),
        check_vma=False,
    )
```

```python
import functools
import math

import jax
import jax.numpy as jnp
import numpy as np
from jax import lax
from jax.experimental import pallas as pl
from jax.experimental.pallas import tpu as pltpu
from jax.sharding import PartitionSpec as P

BF = jnp.bfloat16
F32 = jnp.float32
PARK = {"x1": (0, 2592), "a1": (2592, 1760), "x3": (4352, 1728), "slope1": (0, 1024), "slope2": (1024, 512)}
PARK_SHAPES = ((90112, 384), (67584, 256))


def parked(park, name, lanes):
    first, count = PARK[name]
    return park.at[first:first + count, 0:lanes]


def call(name, body, inputs, far_inputs, outputs, far_outputs=(), scratch=(), limit=24, flops=1 << 28):
    near, far = pl.BlockSpec(memory_space=pltpu.VMEM), pl.BlockSpec(memory_space=pl.ANY)
    return pl.pallas_call(
        body,
        out_shape=(*outputs, *far_outputs),
        in_specs=[near] * len(inputs) + [far] * len(far_inputs),
        out_specs=(near,) * len(outputs) + (far,) * len(far_outputs),
        scratch_shapes=list(scratch),
        compiler_params=pltpu.CompilerParams(vmem_limit_bytes=limit * 1024 * 1024),
        cost_estimate=pl.CostEstimate(flops=flops, bytes_accessed=1 << 20, transcendentals=0),
        name=name,
    )(*inputs, *far_inputs)


def array(dtype, *shape):
    return jax.ShapeDtypeStruct(shape, dtype)


def shifted(block, axis, distance):
    devices = range(lax.axis_size(axis))
    route = [(i - distance, i) for i in devices if i - distance in devices]
    return lax.ppermute(block, axis, route)


def diagonal(block):
    nd, nh = lax.axis_size("dev"), lax.axis_size("ha")
    route = [(i * nh + j, (i + 1) * nh + j + 1) for i in range(nd - 1) for j in range(nh - 1)]
    return lax.ppermute(block, ("dev", "ha"), route)


def mm(left, right):
    return jnp.dot(left, right, preferred_element_type=F32)


def mm_nt(left, right):
    return lax.dot_general(left, right, (((1,), (1,)), ((), ())), preferred_element_type=F32)


def leaky_and_slope(z):
    u = 4.0 * z
    t = jnp.exp(-jnp.abs(u))
    s = 1.0 + t
    act = 0.3 * z + 0.175 * (jnp.maximum(u, 0.0) + jnp.log(s))
    r = 1.0 / s
    slope = 0.3 + 0.7 * jnp.where(u >= 0.0, r, t * r)
    return act, slope


def row_height(r):
    return np.where(r < 64, r % 16, (r - 64) % 8 - 8)


def row_channel(r):
    return np.where(r < 64, r // 16, (r - 64) // 8)


def constants(width):
    s = width // 8
    cols = np.arange(288)
    a, r = cols // 96, cols % 96
    am = a * 4 + row_channel(r)
    j = np.arange(256) // 32
    spread_o = (np.arange(256)[:, None] % 32 == np.arange(32)[None]).astype(np.float32)
    spread_am = (np.arange(16)[:, None] == am[None]).astype(np.float32)
    mask = np.stack([(row_height(r)[:, None] == (2 * j - 1 + b)[None]) for b in range(3)]).astype(np.float32)
    later = np.zeros((2 * s, 2 * s), np.float32)
    for c in range(s):
        later[c, s + c] = 1
        if c + 1 < s:
            later[s + c, c + 1] = 1
    pair = np.zeros((4 * s, 6 * s), np.float32)
    for k in range(2):
        for c in range(s):
            pair[k * 2 * s + c, 2 * s + k * s + c] = 1
            pair[k * 2 * s + s + c, 4 * s + k * s + c] = 1
            if c + 1 < s:
                pair[k * 2 * s + s + c, k * s + c + 1] = 1
    spread = np.zeros((2 * s, 12 * s), np.float32)
    for k in range(2):
        for c in range(s):
            base = k * 6 * s
            spread[k * s + c, base + c] = 1
            spread[k * s + c, base + 2 * s + s + c] = 1
            if c > 0:
                spread[k * s + c, base + 4 * s + s + c - 1] = 1
    return {
        "spread_o": spread_o, "spread_am": spread_am, "mask": mask,
        "later": later, "pair": pair, "spread": spread,
    }


def deinterleave(width):
    s = width // 8
    col = lax.broadcasted_iota(jnp.int32, (1, 12 * s), 1)
    k = col % (4 * s) // s
    source = 8 * (col % s) + 2 * (k % 2 * 2 + k // 2) - 1 + col // (4 * s)
    row = lax.broadcasted_iota(jnp.int32, (width, 12 * s), 0)
    return jnp.where(row == source, 1.0, 0.0).astype(BF)


def plane_taps(j):
    col = lax.broadcasted_iota(jnp.int32, (1, 288), 1)
    a = col // 96
    r = col % 96
    channel = jnp.where(r < 64, r // 16, (r - 64) // 8)
    height = jnp.where(r < 64, r % 16, r % 8 - 8)
    row = lax.broadcasted_iota(jnp.int32, (36, 1), 0)
    want = (row // 12 * 4 + row % 4) * 64 + (2 * j - 1 + row // 4 % 3 + 32)
    return jnp.where(want == (a * 4 + channel) * 64 + (height + 32), 1.0, 0.0).astype(BF)


def prep_body(cot_ref, w3_ref, out_ref):
    nh = out_ref.shape[0]
    cot = cot_ref[...].astype(F32)
    for k in range(14):
        pair = [w3_ref[tap] for tap in (2 * k, 2 * k + 1) if tap < 27]
        pair = jnp.concatenate(pair, 1) if len(pair) > 1 else pair[0]
        for h in range(nh):
            out_ref[h, :, 128 + k * 128:128 + k * 128 + pair.shape[1]] = pair
    for h in range(nh):
        out_ref[h, :, 0:128] = jnp.concatenate([cot[:, 2 * h], cot[:, 2 * h + 1]], 1).astype(BF)


def first_body(*refs):
    sources, refs = refs[:8], refs[8:]
    park_b, park_f = refs[:2]
    held, refs = refs[2:10], refs[10:]
    w1_ref, volume_ref, hz_ref, dd_ref, dz_ref, later_ref, w2_ref, pair_ref = held
    (x1_ref, a1_ref, t_ref, a2_ref, slope1_ref, slope2_ref, x3_ref, sems, came) = refs
    fetches = [pltpu.make_async_copy(sources[i], held[i], came.at[i]) for i in range(8)]
    for fetch in fetches:
        fetch.start()
    sends = []

    def send(source, park, name, first=0):
        rows, lanes = source.shape
        first += PARK[name][0]
        copy = pltpu.make_async_copy(source, park.at[first:first + rows, 0:lanes], sems.at[len(sends)])
        copy.start()
        sends.append(copy)

    low_dev = (lax.axis_index("dev") > 0).astype(F32)
    low_ha = (lax.axis_index("ha") > 0).astype(F32)
    sel = deinterleave(volume_ref.shape[3])
    taps = [plane_taps(j - 3) for j in range(11)]
    fetches[0].wait()
    w1 = w1_ref[...].astype(F32)
    w1 = jnp.concatenate([jnp.concatenate([w1[k * 3 + e] for k in range(9)], 0) for e in range(3)], 1)
    wt = w1.T.astype(BF)
    for j in range(11):
        part = mm(wt, taps[j])
        t_ref[j * 32:j * 32 + 32] = jnp.concatenate([part[0:32], part[32:64], part[64:96]], 1).astype(BF)
    for volume, edges, first, skip, given in ((volume_ref, hz_ref, 7, 0, (1, 2)), (dd_ref, dz_ref, -1, 1, (3, 4))):
        for i in given:
            fetches[i].wait()
        side = mm(edges[...].reshape(256, -1), sel).astype(BF)
        main = [mm(volume[m, skip:].reshape((8 - skip) * 16, -1), sel).astype(BF) for m in range(4)]
        for d in range(skip, 8):
            base = (first + d) * 96
            for e in range(3):
                lanes = slice(e * 256, e * 256 + 256)
                for m in range(4):
                    x1_ref[e, base + m * 16:base + m * 16 + 16] = main[m][(d - skip) * 16:(d - skip) * 16 + 16, lanes]
                x1_ref[e, base + 64:base + 96] = side[d * 32:d * 32 + 32, lanes]
    for e in range(3):
        send(x1_ref.at[e, 576:1440], park_b, "x1", e * 864)
    t = t_ref[...]
    fetches[5].wait()
    later = later_ref[...]
    for ii in range(7):
        lo = ii * 192
        z = mm(t, jnp.concatenate([x1_ref[e, lo:lo + 288] for e in range(3)], 0))
        act, slope = leaky_and_slope(z)
        rows = lax.broadcasted_iota(jnp.int32, act.shape, 0)
        keep = jnp.where(rows < 96, low_ha, 1.0)
        if ii < 3:
            keep = keep * low_dev
        act = (act * keep).astype(BF)
        here = slice(ii * 352, ii * 352 + 352)
        a1_ref[here, 128:384] = act
        a1_ref[here, 0:128] = mm(act[:, 128:256], later).astype(BF)
        if ii >= 3:
            slope1_ref[(ii - 3) * 256:(ii - 2) * 256] = slope[96:352]
    send(a1_ref.at[704:2464], park_b, "a1")
    send(slope1_ref, park_f, "slope1")

    def at(p, a, q, b):
        return (2 * p + a) * 352 + (2 * q + b) * 32

    def patch(p, q):
        return jnp.concatenate(
            [
                a1_ref[at(p + 1, a, q + 1, b):at(p + 1, a, q + 1, b) + 32, e * 128:e * 128 + 128]
                for a in range(3) for b in range(3) for e in range(3)
            ], 0)

    fetches[6].wait()
    w2t = w2_ref[...].astype(F32).T.astype(BF)
    for p in range(-1, 2):
        for group in ((-1, 0), (1, 2), (3,)):
            x = jnp.concatenate([patch(p, q) for q in group], 1)
            act, slope = leaky_and_slope(mm(w2t, x))
            for k, q in enumerate(group):
                part = act[:, k * 128:k * 128 + 128]
                if p < 0:
                    part = part * low_dev
                if q < 0:
                    part = part * low_ha
                a2_ref[p + 1, (q + 1) * 64:(q + 2) * 64] = part.astype(BF)
                if p >= 0 and q >= 0:
                    slope2_ref[p * 256 + q * 64:p * 256 + q * 64 + 64] = slope[:, k * 128:k * 128 + 128]
    send(slope2_ref, park_f, "slope2")
    fetches[7].wait()
    for a in range(3):
        both = jnp.concatenate([a2_ref[a, 0:192], a2_ref[a, 128:320]], 1)
        spread = mm(both, pair_ref[...]).astype(BF)
        for b in range(3):
            for e in range(3):
                at = ((a * 3 + b) * 3 + e) * 64
                x3_ref[at:at + 64] = spread[b * 64:b * 64 + 64, e * 128:e * 128 + 128]
    send(x3_ref, park_b, "x3")
    for copy in sends:
        copy.wait()


def third_body(g3_slices, both_ref, park_b, park_f, d3_ref, kept_ref, given_ref, sz_ref, sd_ref, *refs):
    blocks, (x3_ref, slope2_ref, out_ref, g3_ref, sems) = refs[:-5], refs[-5:]
    fetches = (
        pltpu.make_async_copy(parked(park_b, "x3", 128), x3_ref, sems.at[0]),
        pltpu.make_async_copy(parked(park_f, "slope2", 128), slope2_ref, sems.at[1]),
    )
    for fetch in fetches:
        fetch.start()
    for fetch in fetches:
        fetch.wait()
    x3 = x3_ref[...]
    act, slope = leaky_and_slope(mm(both_ref[:, 128:1856], x3))
    out_ref[...] = act
    nh, (ch, _) = len(blocks), blocks[0].shape
    for k in range(nh):
        owner = (lax.axis_index("ha") + k) % nh
        blocks[k][...] = out_ref[pl.ds(pl.multiple_of(owner * ch, ch), ch)].astype(BF)
    d3 = (both_ref[:, 0:128].astype(F32) * slope).astype(BF)
    d3_ref[...] = d3
    sz_ref[0:128] = d3
    sd_ref[0:128] = d3
    for p in range(2):
        sz_ref[128 + 64 * p:192 + 64 * p] = slope2_ref[256 * p:256 * p + 64].astype(BF)
    sd_ref[128:384] = slope2_ref[0:256].astype(BF)
    slices = 128 // g3_slices
    row = lax.broadcasted_iota(jnp.int32, (128, 1), 0)
    source = row // slices % nh * ch + row // (nh * slices) * slices + row % slices
    order = jnp.where(lax.broadcasted_iota(jnp.int32, (128, 128), 1) == source, 1.0, 0.0).astype(BF)
    ordered = mm(order, d3).astype(BF)
    wide = jnp.concatenate([x3, jnp.zeros((64, 128), BF)], 0)
    g3 = mm_nt(ordered, wide).astype(BF)
    for k in range(14):
        g3_ref[k] = g3[:, k * 128:k * 128 + 128]
    g3_ref[14:16] = jnp.zeros((2, 128, 128), BF)
    core = lax.axis_index("dev") % 2
    kept_ref[...] = g3_ref[pl.ds(core * 8, 8)]
    given_ref[...] = g3_ref[pl.ds(8 - core * 8, 8)]


def collect_body(*refs):
    blocks, out_ref = refs[:-1], refs[-1]
    nh = len(blocks)
    for k in range(nh):
        out_ref[(lax.axis_index("ha") + nh - k) % nh] = blocks[k][...]


def sum_body(g3_ref, msg_ref, out_ref):
    nd, nh = out_ref.shape[0], out_ref.shape[1]
    g3 = [sum(g3_ref[d * nh + h].astype(F32) for d in range(core, nd, 2) for h in range(nh)) for core in range(2)]
    msg = jnp.sum(msg_ref[...].astype(F32), 0)
    rows = g3[0].shape[0] // nh
    for h in range(nh):
        block = jnp.concatenate([half[h * rows:(h + 1) * rows] for half in g3] + [msg], 0).astype(BF)
        for d in range(nd):
            out_ref[d, h] = block


def unpack_body(scales, total_ref, g1_ref, g2_ref, g3_ref):
    n, both, _ = total_ref.shape
    lot = 512 // n
    rows = (both - lot) // 2
    slices = n // 8
    for tap in range(27):
        for s in range(slices):
            lo = tap // 16 * rows
            part = total_ref[tap % 16 // 2 * slices + s, lo:lo + rows, tap % 2 * 64:tap % 2 * 64 + 64]
            g3_ref[tap, s * rows:(s + 1) * rows] = part.astype(F32) * scales[2]
    for k in range(2):
        part = total_ref[0:g2_ref.shape[1], 2 * rows:, k * 64:k * 64 + 64]
        g2_ref[k] = part.astype(F32) * scales[1]
    for block in range(3):
        lots = [total_ref[(432 + block * 16) // lot + i, 2 * rows:].astype(F32) for i in range(16 // lot)]
        part = jnp.concatenate(lots, 0) * scales[0]
        for k in range(4 if block < 2 else 1):
            for a in range(3):
                g1_ref[a * 9 + block * 4 + k] = part[a * 4:a * 4 + 4, k * 32:k * 32 + 32]


def backward_body(
    spread_ref, d3_ref, rz_ref, rd_ref, w3g_ref, w2_ref, later_ref, so_ref, sam_ref, mask_ref,
    park_b, park_f,
    msg_ref, d2_ref, d1_ref, slope2_ref, a1_ref, slope1_ref, x1_ref, sems,
):
    fetches = {}
    for i, (park, name, target) in enumerate(
            ((park_f, "slope2", slope2_ref), (park_b, "a1", a1_ref), (park_f, "slope1", slope1_ref), (park_b, "x1", x1_ref))):
        fetches[name] = pltpu.make_async_copy(parked(park, name, target.shape[1]), target, sems.at[i])
        fetches[name].start()
    spread = spread_ref[...]

    def blocks(pair, last):
        both = mm(pair, spread).astype(BF)
        lone = mm(last, spread[:, 0:384]).astype(BF)
        cols = [both[:, 0:384], both[:, 384:768], lone]
        return jnp.concatenate(
            [jnp.concatenate([c[:, e * 128:e * 128 + 128] for e in range(3)], 0) for c in cols], 1)

    u0 = mm(w3g_ref[192:576], blocks(d3_ref[...], rz_ref[0:128]))
    u1 = mm(w3g_ref[0:384], blocks(rd_ref[0:128], rd_ref[384:512]))
    u = {(0, 1): u0[0:192], (0, 2): u0[192:384], (1, 0): u1[0:192], (1, 1): u1[192:384]}
    fetches["slope2"].wait()
    taps = {0: ((1, 0),), 1: ((2, 0), (0, 1)), 2: ((1, 1),), 3: ((2, 1), (0, 2)), 4: ((1, 2),)}
    for x in range(3):
        for y in range(5):
            back = None
            for a, i in taps[x]:
                for b, j in taps[y]:
                    term = u[(i, a)][b * 64:b * 64 + 64, j * 128:j * 128 + 128]
                    back = term if back is None else back + term
            if x < 2 and y < 4:
                slope = slope2_ref[x * 256 + y * 64:x * 256 + y * 64 + 64]
            elif x < 2:
                slope = rz_ref[128 + 64 * x:192 + 64 * x].astype(F32)
            elif y < 4:
                slope = rd_ref[128 + 64 * y:192 + 64 * y].astype(F32)
            else:
                slope = rd_ref[512:576].astype(F32)
            d2_ref[x, :, y * 128:y * 128 + 128] = (back * slope).astype(BF)

    def at(p, a, q, b):
        return (2 * p + a) * 352 + (2 * q + b) * 32

    def patch(p, q):
        return jnp.concatenate(
            [
                a1_ref[at(p, a, q + 1, b):at(p, a, q + 1, b) + 32, e * 128:e * 128 + 128]
                for a in range(3) for b in range(3) for e in range(3)
            ], 0)

    fetches["a1"].wait()
    g2 = None
    for p in range(2):
        for q in (0, 2):
            x = jnp.concatenate([patch(p, q), patch(p, q + 1)], 1)
            term = mm_nt(x, d2_ref[p, :, q * 128:q * 128 + 256])
            g2 = term if g2 is None else g2 + term
    msg_ref[0:432] = jnp.concatenate([g2[0:432], g2[432:864]], 1).astype(BF)

    taps = w2_ref[...].reshape(9, 3, 32, 64)
    w2e = taps[:, 1].reshape(288, 64)
    w2o = jnp.concatenate([taps[:, 2].reshape(288, 64), taps[:, 0].reshape(288, 64)], 1)
    later = later_ref[...]
    ue, uo = {}, {}
    for p, first, end in ((0, 1, 3), (1, 0, 3), (2, 0, 1)):
        d2 = d2_ref[p]
        moved = jnp.concatenate(
            [mm_nt(d2[:, q * 128:q * 128 + 128], later).astype(BF) for q in range(5)], 1)
        e_part = mm(w2e[first * 96:end * 96], d2)
        o_part = mm(w2o[first * 96:end * 96], jnp.concatenate([d2, moved], 0))
        for a in range(first, end):
            lo = (a - first) * 96
            ue[(p, a)] = e_part[lo:lo + 96]
            uo[(p, a)] = o_part[lo:lo + 96]
    fetches["slope1"].wait()
    for x in range(4):
        for y in range(8):
            if y % 2 == 0:
                y_taps = ((1, y // 2),)
            else:
                y_taps = ((2, y // 2), (0, y // 2 + 1))
            x_taps = ((1, x // 2),) if x % 2 == 0 else ((2, x // 2), (0, x // 2 + 1))
            for k, source in ((0, ue), (1, uo)):
                back = None
                for a, p in x_taps:
                    for b, q in y_taps:
                        term = source[(p, a)][b * 32:b * 32 + 32, q * 128:q * 128 + 128]
                        back = term if back is None else back + term
                slope = slope1_ref[x * 256 + y * 32:x * 256 + y * 32 + 32, k * 128:k * 128 + 128]
                d1_ref[y * 32:y * 32 + 32, x * 256 + k * 128:x * 256 + k * 128 + 128] = (back * slope).astype(BF)

    d1 = d1_ref[...]
    so = so_ref[...]
    sam = sam_ref[...]
    columns = []
    fetches["x1"].wait()
    x = jnp.concatenate(
        [jnp.concatenate([x1_ref[e * 864 + i * 192:e * 864 + i * 192 + 288] for e in range(3)], 0) for i in range(4)], 1)
    wide = mm_nt(x, d1)
    grads = [wide[e * 288:e * 288 + 288] for e in range(3)]
    for b in range(3):
        for e in range(3):
            kept = grads[e] * mask_ref[b].astype(F32)
            high = kept.astype(BF)
            low = (kept - high.astype(F32)).astype(BF)
            columns.append(mm(high, so) + mm(low, so))
    wide = jnp.concatenate(columns, 1)
    high = wide.astype(BF)
    low = (wide - high.astype(F32)).astype(BF)
    g1 = (mm(sam, high) + mm(sam, low)).astype(BF)
    msg_ref[432:512] = jnp.zeros((80, 128), BF)
    msg_ref[432:448] = g1[:, 0:128]
    msg_ref[448:464] = g1[:, 128:256]
    msg_ref[464:480, 0:32] = g1[:, 256:288]


def local(volume, w_first, w_second, w_third, cotangent):
    nd, nh = lax.axis_size("dev"), lax.axis_size("ha")
    depth_total = volume.shape[1] * nd
    height_total = volume.shape[2] * nh
    width = volume.shape[3]
    cells = depth_total * height_total * width
    scale_first, scale_second, scale_third = (1.0 / math.sqrt(cells // 8 ** k) for k in (1, 2, 3))
    const = {k: jnp.asarray(v, BF) for k, v in constants(width).items()}
    vmem = pltpu.VMEM

    edge = volume[:, :, 8:].transpose(1, 0, 2, 3).reshape(8, 32, width)
    dd = shifted(volume, "dev", 1)
    dz = diagonal(edge)
    hz = shifted(edge, "ha", 1)

    ch = 128 // nh
    natural = w_third.transpose(0, 1, 2, 4, 3).reshape(27, ch, 64)
    both, = call("prep", prep_body, [cotangent[:, 0], natural], [], [array(BF, nh, ch, 1856)], limit=8)
    both = lax.all_to_all(both, "ha", 0, 0, tiled=True).reshape(128, 1856)
    w2 = w_second.reshape(864, 64)
    dma = pltpu.SemaphoreType.DMA
    loaded = [w_first.reshape(27, 4, 32), volume, hz, dd, dz, const["later"], w2, const["pair"]]
    park_b, park_f = call(
        "first", first_body,
        [], loaded, [],
        [array(BF, *PARK_SHAPES[0]), array(F32, *PARK_SHAPES[1])],
        [*(vmem(x.shape, BF) for x in loaded),
         vmem((3, 1440, 256), BF), vmem((2464, 384), BF), vmem((352, 864), BF), vmem((3, 320, 128), BF),
         vmem((1024, 256), F32), vmem((512, 128), F32), vmem((1728, 128), BF), dma((7,)), dma((8,))],
        63, 1 << 33)

    n = nd * nh
    d3, kept, given, sz, sd, *blocks = call(
        "third", functools.partial(third_body, nh * (n // 8)), [both], [park_b, park_f],
        [array(BF, 128, 128), array(BF, 8, 128, 128), array(BF, 8, 128, 128), array(BF, 256, 128), array(BF, 384, 128), *[array(BF, ch, 128)] * nh],
        (), [vmem((1728, 128), BF), vmem((512, 128), F32), vmem((128, 128), F32), vmem((16, 128, 128), BF), dma((2,))], 8)

    given = lax.ppermute(given, "dev", [(i, i ^ 1) for i in range(nd)])
    halves = (kept.astype(F32) + given.astype(F32)).astype(BF)
    g3_parts = lax.all_to_all(halves.reshape(n, 1024 // n, 128), ("dev", "ha"), 0, 0, tiled=True)
    rz = shifted(sz, "ha", -1)
    rd = shifted(jnp.concatenate([sd, rz[0:192]], 0), "dev", -1)

    for k in range(1, nh):
        blocks[k] = lax.ppermute(blocks[k], "ha", [(i, (i + k) % nh) for i in range(nh)])
    share, = call("collect", collect_body, blocks, [], [array(BF, nh, ch, 128)], limit=4)
    out_third = share.reshape(nh, ch, 2, 64).transpose(1, 0, 2, 3).reshape(ch, 1, 2 * nh, 64)

    w3g = both[:, 128:].reshape(128, 9, 3, 64).transpose(1, 3, 2, 0)
    w3g = jnp.concatenate([w3g[:, :, 1], w3g[:, :, 2], w3g[:, :, 0]], 2).reshape(576, 384)
    msg, = call(
        "backward", backward_body,
        [const["spread"], d3, rz, rd, w3g, w2, const["later"], const["spread_o"], const["spread_am"], const["mask"]],
        [park_b, park_f], [array(BF, 512, 128)], (),
        [vmem((3, 64, 640), BF), vmem((256, 1024), BF), vmem((512, 128), F32), vmem((1760, 384), BF),
         vmem((1024, 256), F32), vmem((2592, 256), BF), dma((4,))],
        24, 1 << 36)

    g3_parts, msg = lax.optimization_barrier((g3_parts, msg))
    msg_parts = lax.all_to_all(msg.reshape(n, 512 // n, 128), ("dev", "ha"), 0, 0, tiled=True)
    rows = 2048 // n // nh
    slices, = call("sum", sum_body, [g3_parts, msg_parts], [], [array(BF, nd, nh, rows + 512 // n, 128)], limit=8)
    total = lax.all_to_all(slices.reshape(n, rows + 512 // n, 128), ("dev", "ha"), 0, 0, tiled=True)
    scales = (scale_first, scale_second, scale_third)
    g1, g2, g3 = call(
        "unpack", functools.partial(unpack_body, scales), [total], [],
        [array(F32, 27, 4, 32), array(F32, 2, 432 * n // 512, 512 // n, 64), array(F32, 27, 128 // nh, 64)], limit=8)
    grad_first = g1.reshape(3, 3, 3, 4, 32)
    grad_second = g2.reshape(3, 3, 3, 32, 64)
    grad_third = g3.transpose(0, 2, 1).reshape(3, 3, 3, 64, 128 // nh)
    return out_third, grad_first, grad_second, grad_third


def solution(mesh):
    placed = (
        P(None, "dev", "ha", None),
        P(),
        P(),
        P(None, None, None, None, "ha"),
        P("ha", "dev", None, None),
    )
    return jax.shard_map(
        local,
        mesh=mesh,
        in_specs=placed,
        out_specs=(P("ha", "dev", None, None), P(), P(), P(None, None, None, None, "ha")),
        check_vma=False,
    )
```

```python
import functools
import math

import jax
import jax.numpy as jnp
import numpy as np
from jax import lax
from jax.experimental import pallas as pl
from jax.experimental.pallas import tpu as pltpu
from jax.sharding import PartitionSpec as P

BF = jnp.bfloat16
F32 = jnp.float32
PARK = {"x1": (0, 2592), "a1": (2592, 1760), "x3": (4352, 1728), "slope1": (0, 1024), "slope2": (1024, 512)}
PARK_SHAPES = ((90112, 384), (67584, 256))


def parked(park, name, lanes):
    first, count = PARK[name]
    return park.at[first:first + count, 0:lanes]


def call(name, body, inputs, far_inputs, outputs, far_outputs=(), scratch=(), limit=24, flops=1 << 28):
    near, far = pl.BlockSpec(memory_space=pltpu.VMEM), pl.BlockSpec(memory_space=pl.ANY)
    return pl.pallas_call(
        body,
        out_shape=(*outputs, *far_outputs),
        in_specs=[near] * len(inputs) + [far] * len(far_inputs),
        out_specs=(near,) * len(outputs) + (far,) * len(far_outputs),
        scratch_shapes=list(scratch),
        compiler_params=pltpu.CompilerParams(vmem_limit_bytes=limit * 1024 * 1024),
        cost_estimate=pl.CostEstimate(flops=flops, bytes_accessed=1 << 20, transcendentals=0),
        name=name,
    )(*inputs, *far_inputs)


def array(dtype, *shape):
    return jax.ShapeDtypeStruct(shape, dtype)


def shifted(block, axis, distance):
    devices = range(lax.axis_size(axis))
    route = [(i - distance, i) for i in devices if i - distance in devices]
    return lax.ppermute(block, axis, route)


def diagonal(block):
    nd, nh = lax.axis_size("dev"), lax.axis_size("ha")
    route = [(i * nh + j, (i + 1) * nh + j + 1) for i in range(nd - 1) for j in range(nh - 1)]
    return lax.ppermute(block, ("dev", "ha"), route)


def mm(left, right):
    return jnp.dot(left, right, preferred_element_type=F32)


def mm_nt(left, right):
    return lax.dot_general(left, right, (((1,), (1,)), ((), ())), preferred_element_type=F32)


def leaky_and_slope(z):
    u = 4.0 * z
    t = jnp.exp(-jnp.abs(u))
    s = 1.0 + t
    act = 0.3 * z + 0.175 * (jnp.maximum(u, 0.0) + jnp.log(s))
    r = 1.0 / s
    slope = 0.3 + 0.7 * jnp.where(u >= 0.0, r, t * r)
    return act, slope


def row_height(r):
    return np.where(r < 64, r % 16, (r - 64) % 8 - 8)


def row_channel(r):
    return np.where(r < 64, r // 16, (r - 64) // 8)


def constants(width):
    s = width // 8
    cols = np.arange(288)
    a, r = cols // 96, cols % 96
    am = a * 4 + row_channel(r)
    j = np.arange(256) // 32
    spread_o = (np.arange(256)[:, None] % 32 == np.arange(32)[None]).astype(np.float32)
    spread_am = (np.arange(16)[:, None] == am[None]).astype(np.float32)
    mask = np.stack([(row_height(r)[:, None] == (2 * j - 1 + b)[None]) for b in range(3)]).astype(np.float32)
    later = np.zeros((2 * s, 2 * s), np.float32)
    for c in range(s):
        later[c, s + c] = 1
        if c + 1 < s:
            later[s + c, c + 1] = 1
    pair = np.zeros((4 * s, 6 * s), np.float32)
    for k in range(2):
        for c in range(s):
            pair[k * 2 * s + c, 2 * s + k * s + c] = 1
            pair[k * 2 * s + s + c, 4 * s + k * s + c] = 1
            if c + 1 < s:
                pair[k * 2 * s + s + c, k * s + c + 1] = 1
    spread = np.zeros((2 * s, 12 * s), np.float32)
    for k in range(2):
        for c in range(s):
            base = k * 6 * s
            spread[k * s + c, base + c] = 1
            spread[k * s + c, base + 2 * s + s + c] = 1
            if c > 0:
                spread[k * s + c, base + 4 * s + s + c - 1] = 1
    return {
        "spread_o": spread_o, "spread_am": spread_am, "mask": mask,
        "later": later, "pair": pair, "spread": spread,
    }


def deinterleave(width):
    s = width // 8
    col = lax.broadcasted_iota(jnp.int32, (1, 8 * s), 1)
    k = col % (4 * s) // s
    source = 8 * (col % s) + 2 * (k % 2 * 2 + k // 2) + col // (4 * s)
    row = lax.broadcasted_iota(jnp.int32, (width, 8 * s), 0)
    return jnp.where(row == source, 1.0, 0.0).astype(BF)


def plane_taps(j):
    col = lax.broadcasted_iota(jnp.int32, (1, 288), 1)
    a = col // 96
    r = col % 96
    channel = jnp.where(r < 64, r // 16, (r - 64) // 8)
    height = jnp.where(r < 64, r % 16, r % 8 - 8)
    row = lax.broadcasted_iota(jnp.int32, (36, 1), 0)
    want = (row // 12 * 4 + row % 4) * 64 + (2 * j - 1 + row // 4 % 3 + 32)
    return jnp.where(want == (a * 4 + channel) * 64 + (height + 32), 1.0, 0.0).astype(BF)


def prep_body(cot_ref, w3_ref, out_ref):
    nh = out_ref.shape[0]
    cot = cot_ref[...].astype(F32)
    for k in range(14):
        pair = [w3_ref[tap] for tap in (2 * k, 2 * k + 1) if tap < 27]
        pair = jnp.concatenate(pair, 1) if len(pair) > 1 else pair[0]
        for h in range(nh):
            out_ref[h, :, 128 + k * 128:128 + k * 128 + pair.shape[1]] = pair
    for h in range(nh):
        out_ref[h, :, 0:128] = jnp.concatenate([cot[:, 2 * h], cot[:, 2 * h + 1]], 1).astype(BF)


def first_body(*refs):
    sources, refs = refs[:8], refs[8:]
    park_b, park_f = refs[:2]
    held, refs = refs[2:10], refs[10:]
    w1_ref, volume_ref, hz_ref, dd_ref, dz_ref, later_ref, w2_ref, pair_ref = held
    (x1_ref, a1_ref, t_ref, a2_ref, slope1_ref, slope2_ref, x3_ref, sems, came) = refs
    fetches = [pltpu.make_async_copy(sources[i], held[i], came.at[i]) for i in range(8)]
    for fetch in fetches:
        fetch.start()
    sends = []

    def send(source, park, name, first=0):
        rows, lanes = source.shape
        first += PARK[name][0]
        copy = pltpu.make_async_copy(source, park.at[first:first + rows, 0:lanes], sems.at[len(sends)])
        copy.start()
        sends.append(copy)

    low_dev = (lax.axis_index("dev") > 0).astype(F32)
    low_ha = (lax.axis_index("ha") > 0).astype(F32)
    sel = deinterleave(volume_ref.shape[3])
    taps = [plane_taps(j - 3) for j in range(11)]
    fetches[0].wait()
    w1 = w1_ref[...].astype(F32)
    w1 = jnp.concatenate([jnp.concatenate([w1[k * 3 + e] for k in range(9)], 0) for e in range(3)], 1)
    wt = w1.T.astype(BF)
    for j in range(11):
        part = mm(wt, taps[j])
        t_ref[j * 32:j * 32 + 32] = jnp.concatenate([part[0:32], part[32:64], part[64:96]], 1).astype(BF)
    fetches[5].wait()
    later = later_ref[...]
    for volume, edges, first, skip, given in ((volume_ref, hz_ref, 7, 0, (1, 2)), (dd_ref, dz_ref, -1, 1, (3, 4))):
        for i in given:
            fetches[i].wait()
        side = mm(edges[...].reshape(256, -1), sel).astype(BF)
        main = [mm(volume[m, skip:].reshape((8 - skip) * 16, -1), sel).astype(BF) for m in range(4)]
        parts = [(part, mm(part[:, 384:512], later).astype(BF)) for part in (*main, side)]
        for d in range(skip, 8):
            base = (first + d) * 96
            for m, (part, moved) in enumerate(parts):
                size = 16 if m < 4 else 32
                rows = slice(d * 32, d * 32 + 32) if m == 4 else slice((d - skip) * 16, (d - skip) * 16 + 16)
                here = slice(base + m * 16, base + m * 16 + size)
                x1_ref[1, here] = part[rows, 0:256]
                x1_ref[2, here] = part[rows, 256:512]
                x1_ref[0, here, 0:128] = moved[rows]
                x1_ref[0, here, 128:256] = part[rows, 256:384]
    for e in range(3):
        send(x1_ref.at[e, 576:1440], park_b, "x1", e * 864)
    t = t_ref[...]
    for ii in range(7):
        lo = ii * 192
        z = mm(t, jnp.concatenate([x1_ref[e, lo:lo + 288] for e in range(3)], 0))
        act, slope = leaky_and_slope(z)
        rows = lax.broadcasted_iota(jnp.int32, act.shape, 0)
        keep = jnp.where(rows < 96, low_ha, 1.0)
        if ii < 3:
            keep = keep * low_dev
        act = (act * keep).astype(BF)
        here = slice(ii * 352, ii * 352 + 352)
        a1_ref[here, 128:384] = act
        a1_ref[here, 0:128] = mm(act[:, 128:256], later).astype(BF)
        if ii >= 3:
            slope1_ref[(ii - 3) * 256:(ii - 2) * 256] = slope[96:352]
    send(a1_ref.at[704:2464], park_b, "a1")
    send(slope1_ref, park_f, "slope1")

    def at(p, a, q, b):
        return (2 * p + a) * 352 + (2 * q + b) * 32

    def patch(p, q):
        return jnp.concatenate(
            [
                a1_ref[at(p + 1, a, q + 1, b):at(p + 1, a, q + 1, b) + 32, e * 128:e * 128 + 128]
                for a in range(3) for b in range(3) for e in range(3)
            ], 0)

    fetches[6].wait()
    w2t = w2_ref[...].astype(F32).T.astype(BF)
    for p in range(-1, 2):
        for group in ((-1, 0), (1, 2), (3,)):
            x = jnp.concatenate([patch(p, q) for q in group], 1)
            act, slope = leaky_and_slope(mm(w2t, x))
            for k, q in enumerate(group):
                part = act[:, k * 128:k * 128 + 128]
                if p < 0:
                    part = part * low_dev
                if q < 0:
                    part = part * low_ha
                a2_ref[p + 1, (q + 1) * 64:(q + 2) * 64] = part.astype(BF)
                if p >= 0 and q >= 0:
                    slope2_ref[p * 256 + q * 64:p * 256 + q * 64 + 64] = slope[:, k * 128:k * 128 + 128]
    send(slope2_ref, park_f, "slope2")
    fetches[7].wait()
    for a in range(3):
        both = jnp.concatenate([a2_ref[a, 0:192], a2_ref[a, 128:320]], 1)
        spread = mm(both, pair_ref[...]).astype(BF)
        for b in range(3):
            for e in range(3):
                at = ((a * 3 + b) * 3 + e) * 64
                x3_ref[at:at + 64] = spread[b * 64:b * 64 + 64, e * 128:e * 128 + 128]
    send(x3_ref, park_b, "x3")
    for copy in sends:
        copy.wait()


def third_body(g3_slices, both_ref, park_b, park_f, d3_ref, kept_ref, given_ref, sz_ref, sd_ref, *refs):
    blocks, (x3_ref, slope2_ref, out_ref, g3_ref, sems) = refs[:-5], refs[-5:]
    fetches = (
        pltpu.make_async_copy(parked(park_b, "x3", 128), x3_ref, sems.at[0]),
        pltpu.make_async_copy(parked(park_f, "slope2", 128), slope2_ref, sems.at[1]),
    )
    for fetch in fetches:
        fetch.start()
    for fetch in fetches:
        fetch.wait()
    x3 = x3_ref[...]
    act, slope = leaky_and_slope(mm(both_ref[:, 128:1856], x3))
    out_ref[...] = act
    nh, (ch, _) = len(blocks), blocks[0].shape
    for k in range(nh):
        owner = (lax.axis_index("ha") + k) % nh
        blocks[k][...] = out_ref[pl.ds(pl.multiple_of(owner * ch, ch), ch)].astype(BF)
    d3 = (both_ref[:, 0:128].astype(F32) * slope).astype(BF)
    d3_ref[...] = d3
    sz_ref[0:128] = d3
    sd_ref[0:128] = d3
    for p in range(2):
        sz_ref[128 + 64 * p:192 + 64 * p] = slope2_ref[256 * p:256 * p + 64].astype(BF)
    sd_ref[128:384] = slope2_ref[0:256].astype(BF)
    slices = 128 // g3_slices
    row = lax.broadcasted_iota(jnp.int32, (128, 1), 0)
    source = row // slices % nh * ch + row // (nh * slices) * slices + row % slices
    order = jnp.where(lax.broadcasted_iota(jnp.int32, (128, 128), 1) == source, 1.0, 0.0).astype(BF)
    ordered = mm(order, d3).astype(BF)
    wide = jnp.concatenate([x3, jnp.zeros((64, 128), BF)], 0)
    g3 = mm_nt(ordered, wide).astype(BF)
    for k in range(14):
        g3_ref[k] = g3[:, k * 128:k * 128 + 128]
    g3_ref[14:16] = jnp.zeros((2, 128, 128), BF)
    core = lax.axis_index("dev") % 2
    kept_ref[...] = g3_ref[pl.ds(core * 8, 8)]
    given_ref[...] = g3_ref[pl.ds(8 - core * 8, 8)]


def collect_body(*refs):
    blocks, out_ref = refs[:-1], refs[-1]
    nh = len(blocks)
    for k in range(nh):
        out_ref[(lax.axis_index("ha") + nh - k) % nh] = blocks[k][...]


def sum_body(g3_ref, msg_ref, out_ref):
    nd, nh = out_ref.shape[0], out_ref.shape[1]
    g3 = [sum(g3_ref[d * nh + h].astype(F32) for d in range(core, nd, 2) for h in range(nh)) for core in range(2)]
    msg = jnp.sum(msg_ref[...].astype(F32), 0)
    rows = g3[0].shape[0] // nh
    for h in range(nh):
        block = jnp.concatenate([half[h * rows:(h + 1) * rows] for half in g3] + [msg], 0).astype(BF)
        for d in range(nd):
            out_ref[d, h] = block


def unpack_body(scales, total_ref, g1_ref, g2_ref, g3_ref):
    n, both, _ = total_ref.shape
    lot = 512 // n
    rows = (both - lot) // 2
    slices = n // 8
    for tap in range(27):
        for s in range(slices):
            lo = tap // 16 * rows
            part = total_ref[tap % 16 // 2 * slices + s, lo:lo + rows, tap % 2 * 64:tap % 2 * 64 + 64]
            g3_ref[tap, s * rows:(s + 1) * rows] = part.astype(F32) * scales[2]
    for k in range(2):
        part = total_ref[0:g2_ref.shape[1], 2 * rows:, k * 64:k * 64 + 64]
        g2_ref[k] = part.astype(F32) * scales[1]
    for block in range(3):
        lots = [total_ref[(432 + block * 16) // lot + i, 2 * rows:].astype(F32) for i in range(16 // lot)]
        part = jnp.concatenate(lots, 0) * scales[0]
        for k in range(4 if block < 2 else 1):
            for a in range(3):
                g1_ref[a * 9 + block * 4 + k] = part[a * 4:a * 4 + 4, k * 32:k * 32 + 32]


def backward_body(
    spread_ref, d3_ref, rz_ref, rd_ref, w3g_ref, w2_ref, later_ref, so_ref, sam_ref, mask_ref,
    park_b, park_f,
    msg_ref, d2_ref, d1_ref, slope2_ref, a1_ref, slope1_ref, x1_ref, sems,
):
    fetches = {}
    for i, (park, name, target) in enumerate(
            ((park_f, "slope2", slope2_ref), (park_b, "a1", a1_ref), (park_f, "slope1", slope1_ref), (park_b, "x1", x1_ref))):
        fetches[name] = pltpu.make_async_copy(parked(park, name, target.shape[1]), target, sems.at[i])
        fetches[name].start()
    spread = spread_ref[...]

    def blocks(pair, last):
        both = mm(pair, spread).astype(BF)
        lone = mm(last, spread[:, 0:384]).astype(BF)
        cols = [both[:, 0:384], both[:, 384:768], lone]
        return jnp.concatenate(
            [jnp.concatenate([c[:, e * 128:e * 128 + 128] for e in range(3)], 0) for c in cols], 1)

    u0 = mm(w3g_ref[192:576], blocks(d3_ref[...], rz_ref[0:128]))
    u1 = mm(w3g_ref[0:384], blocks(rd_ref[0:128], rd_ref[384:512]))
    u = {(0, 1): u0[0:192], (0, 2): u0[192:384], (1, 0): u1[0:192], (1, 1): u1[192:384]}
    fetches["slope2"].wait()
    taps = {0: ((1, 0),), 1: ((2, 0), (0, 1)), 2: ((1, 1),), 3: ((2, 1), (0, 2)), 4: ((1, 2),)}
    for x in range(3):
        for y in range(5):
            back = None
            for a, i in taps[x]:
                for b, j in taps[y]:
                    term = u[(i, a)][b * 64:b * 64 + 64, j * 128:j * 128 + 128]
                    back = term if back is None else back + term
            if x < 2 and y < 4:
                slope = slope2_ref[x * 256 + y * 64:x * 256 + y * 64 + 64]
            elif x < 2:
                slope = rz_ref[128 + 64 * x:192 + 64 * x].astype(F32)
            elif y < 4:
                slope = rd_ref[128 + 64 * y:192 + 64 * y].astype(F32)
            else:
                slope = rd_ref[512:576].astype(F32)
            d2_ref[x, :, y * 128:y * 128 + 128] = (back * slope).astype(BF)

    def at(p, a, q, b):
        return (2 * p + a) * 352 + (2 * q + b) * 32

    def patch(p, q):
        return jnp.concatenate(
            [
                a1_ref[at(p, a, q + 1, b):at(p, a, q + 1, b) + 32, e * 128:e * 128 + 128]
                for a in range(3) for b in range(3) for e in range(3)
            ], 0)

    fetches["a1"].wait()
    g2 = None
    for p in range(2):
        for q in (0, 2):
            x = jnp.concatenate([patch(p, q), patch(p, q + 1)], 1)
            term = mm_nt(x, d2_ref[p, :, q * 128:q * 128 + 256])
            g2 = term if g2 is None else g2 + term
    msg_ref[0:432] = jnp.concatenate([g2[0:432], g2[432:864]], 1).astype(BF)

    taps = w2_ref[...].reshape(9, 3, 32, 64)
    w2e = taps[:, 1].reshape(288, 64)
    w2o = jnp.concatenate([taps[:, 2].reshape(288, 64), taps[:, 0].reshape(288, 64)], 1)
    later = later_ref[...]
    ue, uo = {}, {}
    for p, first, end in ((0, 1, 3), (1, 0, 3), (2, 0, 1)):
        d2 = d2_ref[p]
        moved = jnp.concatenate(
            [mm_nt(d2[:, q * 128:q * 128 + 128], later).astype(BF) for q in range(5)], 1)
        e_part = mm(w2e[first * 96:end * 96], d2)
        o_part = mm(w2o[first * 96:end * 96], jnp.concatenate([d2, moved], 0))
        for a in range(first, end):
            lo = (a - first) * 96
            ue[(p, a)] = e_part[lo:lo + 96]
            uo[(p, a)] = o_part[lo:lo + 96]
    fetches["slope1"].wait()
    for x in range(4):
        for y in range(8):
            if y % 2 == 0:
                y_taps = ((1, y // 2),)
            else:
                y_taps = ((2, y // 2), (0, y // 2 + 1))
            x_taps = ((1, x // 2),) if x % 2 == 0 else ((2, x // 2), (0, x // 2 + 1))
            for k, source in ((0, ue), (1, uo)):
                back = None
                for a, p in x_taps:
                    for b, q in y_taps:
                        term = source[(p, a)][b * 32:b * 32 + 32, q * 128:q * 128 + 128]
                        back = term if back is None else back + term
                slope = slope1_ref[x * 256 + y * 32:x * 256 + y * 32 + 32, k * 128:k * 128 + 128]
                d1_ref[y * 32:y * 32 + 32, x * 256 + k * 128:x * 256 + k * 128 + 128] = (back * slope).astype(BF)

    d1 = d1_ref[...]
    so = so_ref[...]
    sam = sam_ref[...]
    columns = []
    fetches["x1"].wait()
    x = jnp.concatenate(
        [jnp.concatenate([x1_ref[e * 864 + i * 192:e * 864 + i * 192 + 288] for e in range(3)], 0) for i in range(4)], 1)
    wide = mm_nt(x, d1)
    grads = [wide[e * 288:e * 288 + 288] for e in range(3)]
    for b in range(3):
        for e in range(3):
            kept = grads[e] * mask_ref[b].astype(F32)
            high = kept.astype(BF)
            low = (kept - high.astype(F32)).astype(BF)
            columns.append(mm(high, so) + mm(low, so))
    wide = jnp.concatenate(columns, 1)
    high = wide.astype(BF)
    low = (wide - high.astype(F32)).astype(BF)
    g1 = (mm(sam, high) + mm(sam, low)).astype(BF)
    msg_ref[432:512] = jnp.zeros((80, 128), BF)
    msg_ref[432:448] = g1[:, 0:128]
    msg_ref[448:464] = g1[:, 128:256]
    msg_ref[464:480, 0:32] = g1[:, 256:288]


def local(volume, w_first, w_second, w_third, cotangent):
    nd, nh = lax.axis_size("dev"), lax.axis_size("ha")
    depth_total = volume.shape[1] * nd
    height_total = volume.shape[2] * nh
    width = volume.shape[3]
    cells = depth_total * height_total * width
    scale_first, scale_second, scale_third = (1.0 / math.sqrt(cells // 8 ** k) for k in (1, 2, 3))
    const = {k: jnp.asarray(v, BF) for k, v in constants(width).items()}
    vmem = pltpu.VMEM

    edge = volume[:, :, 8:].transpose(1, 0, 2, 3).reshape(8, 32, width)
    dd = shifted(volume, "dev", 1)
    hz = shifted(edge, "ha", 1)

    ch = 128 // nh
    natural = w_third.transpose(0, 1, 2, 4, 3).reshape(27, ch, 64)
    both, = call("prep", prep_body, [cotangent[:, 0], natural], [], [array(BF, nh, ch, 1856)], limit=8)
    hz, both = lax.optimization_barrier((hz, both))
    dz = shifted(hz, "dev", 1)
    both = lax.all_to_all(both, "ha", 0, 0, tiled=True).reshape(128, 1856)
    w2 = w_second.reshape(864, 64)
    dma = pltpu.SemaphoreType.DMA
    loaded = [w_first.reshape(27, 4, 32), volume, hz, dd, dz, const["later"], w2, const["pair"]]
    park_b, park_f = call(
        "first", first_body,
        [], loaded, [],
        [array(BF, *PARK_SHAPES[0]), array(F32, *PARK_SHAPES[1])],
        [*(vmem(x.shape, BF) for x in loaded),
         vmem((3, 1440, 256), BF), vmem((2464, 384), BF), vmem((352, 864), BF), vmem((3, 320, 128), BF),
         vmem((1024, 256), F32), vmem((512, 128), F32), vmem((1728, 128), BF), dma((7,)), dma((8,))],
        63, 1 << 33)

    n = nd * nh
    d3, kept, given, sz, sd, *blocks = call(
        "third", functools.partial(third_body, nh * (n // 8)), [both], [park_b, park_f],
        [array(BF, 128, 128), array(BF, 8, 128, 128), array(BF, 8, 128, 128), array(BF, 256, 128), array(BF, 384, 128), *[array(BF, ch, 128)] * nh],
        (), [vmem((1728, 128), BF), vmem((512, 128), F32), vmem((128, 128), F32), vmem((16, 128, 128), BF), dma((2,))], 8)

    given = lax.ppermute(given, "dev", [(i, i ^ 1) for i in range(nd)])
    halves = (kept.astype(F32) + given.astype(F32)).astype(BF)
    g3_parts = lax.all_to_all(halves.reshape(n, 1024 // n, 128), ("dev", "ha"), 0, 0, tiled=True)
    rz = shifted(sz, "ha", -1)
    rd = shifted(jnp.concatenate([sd, rz[0:192]], 0), "dev", -1)

    for k in range(1, nh):
        blocks[k] = lax.ppermute(blocks[k], "ha", [(i, (i + k) % nh) for i in range(nh)])
    share, = call("collect", collect_body, blocks, [], [array(BF, nh, ch, 128)], limit=4)
    out_third = share.reshape(nh, ch, 2, 64).transpose(1, 0, 2, 3).reshape(ch, 1, 2 * nh, 64)

    w3g = both[:, 128:].reshape(128, 9, 3, 64).transpose(1, 3, 2, 0)
    w3g = jnp.concatenate([w3g[:, :, 1], w3g[:, :, 2], w3g[:, :, 0]], 2).reshape(576, 384)
    msg, = call(
        "backward", backward_body,
        [const["spread"], d3, rz, rd, w3g, w2, const["later"], const["spread_o"], const["spread_am"], const["mask"]],
        [park_b, park_f], [array(BF, 512, 128)], (),
        [vmem((3, 64, 640), BF), vmem((256, 1024), BF), vmem((512, 128), F32), vmem((1760, 384), BF),
         vmem((1024, 256), F32), vmem((2592, 256), BF), dma((4,))],
        24, 1 << 36)

    g3_parts, msg = lax.optimization_barrier((g3_parts, msg))
    msg_parts = lax.all_to_all(msg.reshape(n, 512 // n, 128), ("dev", "ha"), 0, 0, tiled=True)
    rows = 2048 // n // nh
    slices, = call("sum", sum_body, [g3_parts, msg_parts], [], [array(BF, nd, nh, rows + 512 // n, 128)], limit=8)
    total = lax.all_to_all(slices.reshape(n, rows + 512 // n, 128), ("dev", "ha"), 0, 0, tiled=True)
    scales = (scale_first, scale_second, scale_third)
    g1, g2, g3 = call(
        "unpack", functools.partial(unpack_body, scales), [total], [],
        [array(F32, 27, 4, 32), array(F32, 2, 432 * n // 512, 512 // n, 64), array(F32, 27, 128 // nh, 64)], limit=8)
    grad_first = g1.reshape(3, 3, 3, 4, 32)
    grad_second = g2.reshape(3, 3, 3, 32, 64)
    grad_third = g3.transpose(0, 2, 1).reshape(3, 3, 3, 64, 128 // nh)
    return out_third, grad_first, grad_second, grad_third


def solution(mesh):
    placed = (
        P(None, "dev", "ha", None),
        P(),
        P(),
        P(None, None, None, None, "ha"),
        P("ha", "dev", None, None),
    )
    return jax.shard_map(
        local,
        mesh=mesh,
        in_specs=placed,
        out_specs=(P("ha", "dev", None, None), P(), P(), P(None, None, None, None, "ha")),
        check_vma=False,
    )
```

```python
import functools
import math

import jax
import jax.numpy as jnp
import numpy as np
from jax import lax
from jax.experimental import pallas as pl
from jax.experimental.pallas import tpu as pltpu
from jax.sharding import PartitionSpec as P

BF = jnp.bfloat16
F32 = jnp.float32
PARK = {"x1": (0, 2592), "a1": (2592, 1760), "x3": (4352, 1728), "slope1": (0, 1024), "slope2": (1024, 512)}
PARK_SHAPES = ((90112, 384), (67584, 256))


def parked(park, name, lanes):
    first, count = PARK[name]
    return park.at[first:first + count, 0:lanes]


def call(name, body, inputs, far_inputs, outputs, far_outputs=(), scratch=(), limit=24, flops=1 << 28):
    near, far = pl.BlockSpec(memory_space=pltpu.VMEM), pl.BlockSpec(memory_space=pl.ANY)
    return pl.pallas_call(
        body,
        out_shape=(*outputs, *far_outputs),
        in_specs=[near] * len(inputs) + [far] * len(far_inputs),
        out_specs=(near,) * len(outputs) + (far,) * len(far_outputs),
        scratch_shapes=list(scratch),
        compiler_params=pltpu.CompilerParams(vmem_limit_bytes=limit * 1024 * 1024),
        cost_estimate=pl.CostEstimate(flops=flops, bytes_accessed=1 << 20, transcendentals=0),
        name=name,
    )(*inputs, *far_inputs)


def array(dtype, *shape):
    return jax.ShapeDtypeStruct(shape, dtype)


def shifted(block, axis, distance):
    devices = range(lax.axis_size(axis))
    route = [(i - distance, i) for i in devices if i - distance in devices]
    return lax.ppermute(block, axis, route)


def diagonal(block):
    nd, nh = lax.axis_size("dev"), lax.axis_size("ha")
    route = [(i * nh + j, (i + 1) * nh + j + 1) for i in range(nd - 1) for j in range(nh - 1)]
    return lax.ppermute(block, ("dev", "ha"), route)


def mm(left, right):
    return jnp.dot(left, right, preferred_element_type=F32)


def mm_nt(left, right):
    return lax.dot_general(left, right, (((1,), (1,)), ((), ())), preferred_element_type=F32)


def leaky_and_slope(z):
    u = 4.0 * z
    t = jnp.exp(-jnp.abs(u))
    s = 1.0 + t
    act = 0.3 * z + 0.175 * (jnp.maximum(u, 0.0) + jnp.log(s))
    r = 1.0 / s
    slope = 0.3 + 0.7 * jnp.where(u >= 0.0, r, t * r)
    return act, slope


def row_height(r):
    return np.where(r < 64, r % 16, (r - 64) % 8 - 8)


def row_channel(r):
    return np.where(r < 64, r // 16, (r - 64) // 8)


def constants(width):
    s = width // 8
    cols = np.arange(288)
    a, r = cols // 96, cols % 96
    am = a * 4 + row_channel(r)
    j = np.arange(256) // 32
    spread_o = (np.arange(256)[:, None] % 32 == np.arange(32)[None]).astype(np.float32)
    spread_am = (np.arange(16)[:, None] == am[None]).astype(np.float32)
    mask = np.stack([(row_height(r)[:, None] == (2 * j - 1 + b)[None]) for b in range(3)]).astype(np.float32)
    later = np.zeros((2 * s, 2 * s), np.float32)
    for c in range(s):
        later[c, s + c] = 1
        if c + 1 < s:
            later[s + c, c + 1] = 1
    pair = np.zeros((4 * s, 6 * s), np.float32)
    for k in range(2):
        for c in range(s):
            pair[k * 2 * s + c, 2 * s + k * s + c] = 1
            pair[k * 2 * s + s + c, 4 * s + k * s + c] = 1
            if c + 1 < s:
                pair[k * 2 * s + s + c, k * s + c + 1] = 1
    spread = np.zeros((2 * s, 12 * s), np.float32)
    for k in range(2):
        for c in range(s):
            base = k * 6 * s
            spread[k * s + c, base + c] = 1
            spread[k * s + c, base + 2 * s + s + c] = 1
            if c > 0:
                spread[k * s + c, base + 4 * s + s + c - 1] = 1
    return {
        "spread_o": spread_o, "spread_am": spread_am, "mask": mask,
        "later": later, "pair": pair, "spread": spread,
    }


def deinterleave(width):
    s = width // 8
    col = lax.broadcasted_iota(jnp.int32, (1, 12 * s), 1)
    k = col % (4 * s) // s
    source = 8 * (col % s) + 2 * (k % 2 * 2 + k // 2) - 1 + col // (4 * s)
    row = lax.broadcasted_iota(jnp.int32, (width, 12 * s), 0)
    return jnp.where(row == source, 1.0, 0.0).astype(BF)


def plane_taps(j):
    col = lax.broadcasted_iota(jnp.int32, (1, 288), 1)
    a = col // 96
    r = col % 96
    channel = jnp.where(r < 64, r // 16, (r - 64) // 8)
    height = jnp.where(r < 64, r % 16, r % 8 - 8)
    row = lax.broadcasted_iota(jnp.int32, (36, 1), 0)
    want = (row // 12 * 4 + row % 4) * 64 + (2 * j - 1 + row // 4 % 3 + 32)
    return jnp.where(want == (a * 4 + channel) * 64 + (height + 32), 1.0, 0.0).astype(BF)


def prep_body(cot_ref, w3_ref, out_ref):
    nh = out_ref.shape[0]
    cot = cot_ref[...].astype(F32)
    for k in range(14):
        pair = [w3_ref[tap] for tap in (2 * k, 2 * k + 1) if tap < 27]
        pair = jnp.concatenate(pair, 1) if len(pair) > 1 else pair[0]
        for h in range(nh):
            out_ref[h, :, 128 + k * 128:128 + k * 128 + pair.shape[1]] = pair
    for h in range(nh):
        out_ref[h, :, 0:128] = jnp.concatenate([cot[:, 2 * h], cot[:, 2 * h + 1]], 1).astype(BF)


def first_body(*refs):
    sources, refs = refs[:8], refs[8:]
    park_b, park_f = refs[:2]
    held, refs = refs[2:10], refs[10:]
    w1_ref, volume_ref, hz_ref, dd_ref, dz_ref, later_ref, w2_ref, pair_ref = held
    (x1_ref, a1_ref, t_ref, a2_ref, slope1_ref, slope2_ref, x3_ref, sems, came) = refs
    fetches = [pltpu.make_async_copy(sources[i], held[i], came.at[i]) for i in range(8)]
    for fetch in fetches:
        fetch.start()
    sends = []

    def send(source, park, name, first=0):
        rows, lanes = source.shape
        first += PARK[name][0]
        copy = pltpu.make_async_copy(source, park.at[first:first + rows, 0:lanes], sems.at[len(sends)])
        copy.start()
        sends.append(copy)

    low_dev = (lax.axis_index("dev") > 0).astype(F32)
    low_ha = (lax.axis_index("ha") > 0).astype(F32)
    sel = deinterleave(volume_ref.shape[3])
    taps = [plane_taps(j - 3) for j in range(11)]
    fetches[0].wait()
    w1 = w1_ref[...].astype(F32)
    w1 = jnp.concatenate([jnp.concatenate([w1[k * 3 + e] for k in range(9)], 0) for e in range(3)], 1)
    wt = w1.T.astype(BF)
    for j in range(11):
        part = mm(wt, taps[j])
        t_ref[j * 32:j * 32 + 32] = jnp.concatenate([part[0:32], part[32:64], part[64:96]], 1).astype(BF)
    for volume, edges, first, skip, given in ((volume_ref, hz_ref, 7, 0, (1, 2)), (dd_ref, dz_ref, -1, 1, (3, 4))):
        for i in given:
            fetches[i].wait()
        side = mm(edges[...].reshape(256, -1), sel).astype(BF)
        main = [mm(volume[m, skip:].reshape((8 - skip) * 16, -1), sel).astype(BF) for m in range(4)]
        for d in range(skip, 8):
            base = (first + d) * 96
            for e in range(3):
                lanes = slice(e * 256, e * 256 + 256)
                for m in range(4):
                    x1_ref[e, base + m * 16:base + m * 16 + 16] = main[m][(d - skip) * 16:(d - skip) * 16 + 16, lanes]
                x1_ref[e, base + 64:base + 96] = side[d * 32:d * 32 + 32, lanes]
    for e in range(3):
        send(x1_ref.at[e, 576:1440], park_b, "x1", e * 864)
    t = t_ref[...]
    fetches[5].wait()
    later = later_ref[...]
    for ii in range(7):
        lo = ii * 192
        z = mm(t, jnp.concatenate([x1_ref[e, lo:lo + 288] for e in range(3)], 0))
        act, slope = leaky_and_slope(z)
        rows = lax.broadcasted_iota(jnp.int32, act.shape, 0)
        keep = jnp.where(rows < 96, low_ha, 1.0)
        if ii < 3:
            keep = keep * low_dev
        act = (act * keep).astype(BF)
        here = slice(ii * 352, ii * 352 + 352)
        a1_ref[here, 128:384] = act
        a1_ref[here, 0:128] = mm(act[:, 128:256], later).astype(BF)
        if ii >= 3:
            slope1_ref[(ii - 3) * 256:(ii - 2) * 256] = slope[96:352]
    send(a1_ref.at[704:2464], park_b, "a1")
    send(slope1_ref, park_f, "slope1")

    def at(p, a, q, b):
        return (2 * p + a) * 352 + (2 * q + b) * 32

    def patch(p, q):
        return jnp.concatenate(
            [
                a1_ref[at(p + 1, a, q + 1, b):at(p + 1, a, q + 1, b) + 32, e * 128:e * 128 + 128]
                for a in range(3) for b in range(3) for e in range(3)
            ], 0)

    fetches[6].wait()
    w2t = w2_ref[...].astype(F32).T.astype(BF)
    for p in range(-1, 2):
        for group in ((-1, 0), (1, 2), (3,)):
            x = jnp.concatenate([patch(p, q) for q in group], 1)
            act, slope = leaky_and_slope(mm(w2t, x))
            for k, q in enumerate(group):
                part = act[:, k * 128:k * 128 + 128]
                if p < 0:
                    part = part * low_dev
                if q < 0:
                    part = part * low_ha
                a2_ref[p + 1, (q + 1) * 64:(q + 2) * 64] = part.astype(BF)
                if p >= 0 and q >= 0:
                    slope2_ref[p * 256 + q * 64:p * 256 + q * 64 + 64] = slope[:, k * 128:k * 128 + 128]
    send(slope2_ref, park_f, "slope2")
    fetches[7].wait()
    for a in range(3):
        both = jnp.concatenate([a2_ref[a, 0:192], a2_ref[a, 128:320]], 1)
        spread = mm(both, pair_ref[...]).astype(BF)
        for b in range(3):
            for e in range(3):
                at = ((a * 3 + b) * 3 + e) * 64
                x3_ref[at:at + 64] = spread[b * 64:b * 64 + 64, e * 128:e * 128 + 128]
    send(x3_ref, park_b, "x3")
    for copy in sends:
        copy.wait()


def third_body(both_ref, park_b, park_f, d3_ref, sz_ref, sd_ref, *refs):
    blocks, (x3_ref, slope2_ref, out_ref, sems) = refs[:-4], refs[-4:]
    fetches = (
        pltpu.make_async_copy(parked(park_b, "x3", 128), x3_ref, sems.at[0]),
        pltpu.make_async_copy(parked(park_f, "slope2", 128), slope2_ref, sems.at[1]),
    )
    for fetch in fetches:
        fetch.start()
    for fetch in fetches:
        fetch.wait()
    x3 = x3_ref[...]
    act, slope = leaky_and_slope(mm(both_ref[:, 128:1856], x3))
    out_ref[...] = act
    nh, (ch, _) = len(blocks), blocks[0].shape
    for k in range(nh):
        owner = (lax.axis_index("ha") + k) % nh
        blocks[k][...] = out_ref[pl.ds(pl.multiple_of(owner * ch, ch), ch)].astype(BF)
    d3 = (both_ref[:, 0:128].astype(F32) * slope).astype(BF)
    d3_ref[...] = d3
    sz_ref[0:128] = d3
    sd_ref[0:128] = d3
    for p in range(2):
        sz_ref[128 + 64 * p:192 + 64 * p] = slope2_ref[256 * p:256 * p + 64].astype(BF)
    sd_ref[128:384] = slope2_ref[0:256].astype(BF)


def third_grad_body(g3_slices, nh, d3_ref, park_b, kept_ref, given_ref, x3_ref, g3_ref, sems):
    fetch = pltpu.make_async_copy(parked(park_b, "x3", 128), x3_ref, sems.at[0])
    fetch.start()
    ch = 128 // nh
    d3 = d3_ref[...]
    slices = 128 // g3_slices
    row = lax.broadcasted_iota(jnp.int32, (128, 1), 0)
    source = row // slices % nh * ch + row // (nh * slices) * slices + row % slices
    order = jnp.where(lax.broadcasted_iota(jnp.int32, (128, 128), 1) == source, 1.0, 0.0).astype(BF)
    ordered = mm(order, d3).astype(BF)
    fetch.wait()
    wide = jnp.concatenate([x3_ref[...], jnp.zeros((64, 128), BF)], 0)
    g3 = mm_nt(ordered, wide).astype(BF)
    for k in range(14):
        g3_ref[k] = g3[:, k * 128:k * 128 + 128]
    g3_ref[14:16] = jnp.zeros((2, 128, 128), BF)
    core = lax.axis_index("dev") % 2
    kept_ref[...] = g3_ref[pl.ds(core * 8, 8)]
    given_ref[...] = g3_ref[pl.ds(8 - core * 8, 8)]


def collect_body(*refs):
    blocks, out_ref = refs[:-1], refs[-1]
    nh = len(blocks)
    for k in range(nh):
        out_ref[(lax.axis_index("ha") + nh - k) % nh] = blocks[k][...]


def sum_body(g3_ref, msg_ref, out_ref):
    nd, nh = out_ref.shape[0], out_ref.shape[1]
    g3 = [sum(g3_ref[d * nh + h].astype(F32) for d in range(core, nd, 2) for h in range(nh)) for core in range(2)]
    msg = jnp.sum(msg_ref[...].astype(F32), 0)
    rows = g3[0].shape[0] // nh
    for h in range(nh):
        block = jnp.concatenate([half[h * rows:(h + 1) * rows] for half in g3] + [msg], 0).astype(BF)
        for d in range(nd):
            out_ref[d, h] = block


def unpack_body(scales, total_ref, g1_ref, g2_ref, g3_ref):
    n, both, _ = total_ref.shape
    lot = 512 // n
    rows = (both - lot) // 2
    slices = n // 8
    for tap in range(27):
        for s in range(slices):
            lo = tap // 16 * rows
            part = total_ref[tap % 16 // 2 * slices + s, lo:lo + rows, tap % 2 * 64:tap % 2 * 64 + 64]
            g3_ref[tap, s * rows:(s + 1) * rows] = part.astype(F32) * scales[2]
    for k in range(2):
        part = total_ref[0:g2_ref.shape[1], 2 * rows:, k * 64:k * 64 + 64]
        g2_ref[k] = part.astype(F32) * scales[1]
    for block in range(3):
        lots = [total_ref[(432 + block * 16) // lot + i, 2 * rows:].astype(F32) for i in range(16 // lot)]
        part = jnp.concatenate(lots, 0) * scales[0]
        for k in range(4 if block < 2 else 1):
            for a in range(3):
                g1_ref[a * 9 + block * 4 + k] = part[a * 4:a * 4 + 4, k * 32:k * 32 + 32]


def backward_body(
    spread_ref, d3_ref, rz_ref, rd_ref, w3g_ref, w2_ref, later_ref, so_ref, sam_ref, mask_ref,
    park_b, park_f,
    msg_ref, d2_ref, d1_ref, slope2_ref, a1_ref, slope1_ref, x1_ref, sems,
):
    fetches = {}
    for i, (park, name, target) in enumerate(
            ((park_f, "slope2", slope2_ref), (park_b, "a1", a1_ref), (park_f, "slope1", slope1_ref), (park_b, "x1", x1_ref))):
        fetches[name] = pltpu.make_async_copy(parked(park, name, target.shape[1]), target, sems.at[i])
        fetches[name].start()
    spread = spread_ref[...]

    def blocks(pair, last):
        both = mm(pair, spread).astype(BF)
        lone = mm(last, spread[:, 0:384]).astype(BF)
        cols = [both[:, 0:384], both[:, 384:768], lone]
        return jnp.concatenate(
            [jnp.concatenate([c[:, e * 128:e * 128 + 128] for e in range(3)], 0) for c in cols], 1)

    u0 = mm(w3g_ref[192:576], blocks(d3_ref[...], rz_ref[0:128]))
    u1 = mm(w3g_ref[0:384], blocks(rd_ref[0:128], rd_ref[384:512]))
    u = {(0, 1): u0[0:192], (0, 2): u0[192:384], (1, 0): u1[0:192], (1, 1): u1[192:384]}
    fetches["slope2"].wait()
    taps = {0: ((1, 0),), 1: ((2, 0), (0, 1)), 2: ((1, 1),), 3: ((2, 1), (0, 2)), 4: ((1, 2),)}
    for x in range(3):
        for y in range(5):
            back = None
            for a, i in taps[x]:
                for b, j in taps[y]:
                    term = u[(i, a)][b * 64:b * 64 + 64, j * 128:j * 128 + 128]
                    back = term if back is None else back + term
            if x < 2 and y < 4:
                slope = slope2_ref[x * 256 + y * 64:x * 256 + y * 64 + 64]
            elif x < 2:
                slope = rz_ref[128 + 64 * x:192 + 64 * x].astype(F32)
            elif y < 4:
                slope = rd_ref[128 + 64 * y:192 + 64 * y].astype(F32)
            else:
                slope = rd_ref[512:576].astype(F32)
            d2_ref[x, :, y * 128:y * 128 + 128] = (back * slope).astype(BF)

    def at(p, a, q, b):
        return (2 * p + a) * 352 + (2 * q + b) * 32

    def patch(p, q):
        return jnp.concatenate(
            [
                a1_ref[at(p, a, q + 1, b):at(p, a, q + 1, b) + 32, e * 128:e * 128 + 128]
                for a in range(3) for b in range(3) for e in range(3)
            ], 0)

    fetches["a1"].wait()
    g2 = None
    for p in range(2):
        for q in (0, 2):
            x = jnp.concatenate([patch(p, q), patch(p, q + 1)], 1)
            term = mm_nt(x, d2_ref[p, :, q * 128:q * 128 + 256])
            g2 = term if g2 is None else g2 + term
    msg_ref[0:432] = jnp.concatenate([g2[0:432], g2[432:864]], 1).astype(BF)

    taps = w2_ref[...].reshape(9, 3, 32, 64)
    w2e = taps[:, 1].reshape(288, 64)
    w2o = jnp.concatenate([taps[:, 2].reshape(288, 64), taps[:, 0].reshape(288, 64)], 1)
    later = later_ref[...]
    ue, uo = {}, {}
    for p, first, end in ((0, 1, 3), (1, 0, 3), (2, 0, 1)):
        d2 = d2_ref[p]
        moved = jnp.concatenate(
            [mm_nt(d2[:, q * 128:q * 128 + 128], later).astype(BF) for q in range(5)], 1)
        e_part = mm(w2e[first * 96:end * 96], d2)
        o_part = mm(w2o[first * 96:end * 96], jnp.concatenate([d2, moved], 0))
        for a in range(first, end):
            lo = (a - first) * 96
            ue[(p, a)] = e_part[lo:lo + 96]
            uo[(p, a)] = o_part[lo:lo + 96]
    fetches["slope1"].wait()
    for x in range(4):
        for y in range(8):
            if y % 2 == 0:
                y_taps = ((1, y // 2),)
            else:
                y_taps = ((2, y // 2), (0, y // 2 + 1))
            x_taps = ((1, x // 2),) if x % 2 == 0 else ((2, x // 2), (0, x // 2 + 1))
            for k, source in ((0, ue), (1, uo)):
                back = None
                for a, p in x_taps:
                    for b, q in y_taps:
                        term = source[(p, a)][b * 32:b * 32 + 32, q * 128:q * 128 + 128]
                        back = term if back is None else back + term
                slope = slope1_ref[x * 256 + y * 32:x * 256 + y * 32 + 32, k * 128:k * 128 + 128]
                d1_ref[y * 32:y * 32 + 32, x * 256 + k * 128:x * 256 + k * 128 + 128] = (back * slope).astype(BF)

    d1 = d1_ref[...]
    so = so_ref[...]
    sam = sam_ref[...]
    columns = []
    fetches["x1"].wait()
    x = jnp.concatenate(
        [jnp.concatenate([x1_ref[e * 864 + i * 192:e * 864 + i * 192 + 288] for e in range(3)], 0) for i in range(4)], 1)
    wide = mm_nt(x, d1)
    grads = [wide[e * 288:e * 288 + 288] for e in range(3)]
    for b in range(3):
        for e in range(3):
            kept = grads[e] * mask_ref[b].astype(F32)
            high = kept.astype(BF)
            low = (kept - high.astype(F32)).astype(BF)
            columns.append(mm(high, so) + mm(low, so))
    wide = jnp.concatenate(columns, 1)
    high = wide.astype(BF)
    low = (wide - high.astype(F32)).astype(BF)
    g1 = (mm(sam, high) + mm(sam, low)).astype(BF)
    msg_ref[432:512] = jnp.zeros((80, 128), BF)
    msg_ref[432:448] = g1[:, 0:128]
    msg_ref[448:464] = g1[:, 128:256]
    msg_ref[464:480, 0:32] = g1[:, 256:288]


def local(volume, w_first, w_second, w_third, cotangent):
    nd, nh = lax.axis_size("dev"), lax.axis_size("ha")
    depth_total = volume.shape[1] * nd
    height_total = volume.shape[2] * nh
    width = volume.shape[3]
    cells = depth_total * height_total * width
    scale_first, scale_second, scale_third = (1.0 / math.sqrt(cells // 8 ** k) for k in (1, 2, 3))
    const = {k: jnp.asarray(v, BF) for k, v in constants(width).items()}
    vmem = pltpu.VMEM

    edge = volume[:, :, 8:].transpose(1, 0, 2, 3).reshape(8, 32, width)
    dd = shifted(volume, "dev", 1)
    dz = diagonal(edge)
    hz = shifted(edge, "ha", 1)

    ch = 128 // nh
    natural = w_third.transpose(0, 1, 2, 4, 3).reshape(27, ch, 64)
    both, = call("prep", prep_body, [cotangent[:, 0], natural], [], [array(BF, nh, ch, 1856)], limit=8)
    both = lax.all_to_all(both, "ha", 0, 0, tiled=True).reshape(128, 1856)
    w2 = w_second.reshape(864, 64)
    dma = pltpu.SemaphoreType.DMA
    loaded = [w_first.reshape(27, 4, 32), volume, hz, dd, dz, const["later"], w2, const["pair"]]
    park_b, park_f = call(
        "first", first_body,
        [], loaded, [],
        [array(BF, *PARK_SHAPES[0]), array(F32, *PARK_SHAPES[1])],
        [*(vmem(x.shape, BF) for x in loaded),
         vmem((3, 1440, 256), BF), vmem((2464, 384), BF), vmem((352, 864), BF), vmem((3, 320, 128), BF),
         vmem((1024, 256), F32), vmem((512, 128), F32), vmem((1728, 128), BF), dma((7,)), dma((8,))],
        63, 1 << 33)

    n = nd * nh
    d3, sz, sd, *blocks = call(
        "third", third_body, [both], [park_b, park_f],
        [array(BF, 128, 128), array(BF, 256, 128), array(BF, 384, 128), *[array(BF, ch, 128)] * nh],
        (), [vmem((1728, 128), BF), vmem((512, 128), F32), vmem((128, 128), F32), dma((2,))], 8)
    kept, given = call(
        "third_grad", functools.partial(third_grad_body, nh * (n // 8), nh), [d3], [park_b],
        [array(BF, 8, 128, 128), array(BF, 8, 128, 128)],
        (), [vmem((1728, 128), BF), vmem((16, 128, 128), BF), dma((1,))], 8, 1 << 32)

    given = lax.ppermute(given, "dev", [(i, i ^ 1) for i in range(nd)])
    halves = (kept.astype(F32) + given.astype(F32)).astype(BF)
    g3_parts = lax.all_to_all(halves.reshape(n, 1024 // n, 128), ("dev", "ha"), 0, 0, tiled=True)
    rz = shifted(sz, "ha", -1)
    rd = shifted(jnp.concatenate([sd, rz[0:192]], 0), "dev", -1)

    for k in range(1, nh):
        blocks[k] = lax.ppermute(blocks[k], "ha", [(i, (i + k) % nh) for i in range(nh)])
    share, = call("collect", collect_body, blocks, [], [array(BF, nh, ch, 128)], limit=4)
    out_third = share.reshape(nh, ch, 2, 64).transpose(1, 0, 2, 3).reshape(ch, 1, 2 * nh, 64)

    w3g = both[:, 128:].reshape(128, 9, 3, 64).transpose(1, 3, 2, 0)
    w3g = jnp.concatenate([w3g[:, :, 1], w3g[:, :, 2], w3g[:, :, 0]], 2).reshape(576, 384)
    msg, = call(
        "backward", backward_body,
        [const["spread"], d3, rz, rd, w3g, w2, const["later"], const["spread_o"], const["spread_am"], const["mask"]],
        [park_b, park_f], [array(BF, 512, 128)], (),
        [vmem((3, 64, 640), BF), vmem((256, 1024), BF), vmem((512, 128), F32), vmem((1760, 384), BF),
         vmem((1024, 256), F32), vmem((2592, 256), BF), dma((4,))],
        24, 1 << 36)

    g3_parts, msg = lax.optimization_barrier((g3_parts, msg))
    msg_parts = lax.all_to_all(msg.reshape(n, 512 // n, 128), ("dev", "ha"), 0, 0, tiled=True)
    rows = 2048 // n // nh
    slices, = call("sum", sum_body, [g3_parts, msg_parts], [], [array(BF, nd, nh, rows + 512 // n, 128)], limit=8)
    total = lax.all_to_all(slices.reshape(n, rows + 512 // n, 128), ("dev", "ha"), 0, 0, tiled=True)
    scales = (scale_first, scale_second, scale_third)
    g1, g2, g3 = call(
        "unpack", functools.partial(unpack_body, scales), [total], [],
        [array(F32, 27, 4, 32), array(F32, 2, 432 * n // 512, 512 // n, 64), array(F32, 27, 128 // nh, 64)], limit=8)
    grad_first = g1.reshape(3, 3, 3, 4, 32)
    grad_second = g2.reshape(3, 3, 3, 32, 64)
    grad_third = g3.transpose(0, 2, 1).reshape(3, 3, 3, 64, 128 // nh)
    return out_third, grad_first, grad_second, grad_third


def solution(mesh):
    placed = (
        P(None, "dev", "ha", None),
        P(),
        P(),
        P(None, None, None, None, "ha"),
        P("ha", "dev", None, None),
    )
    return jax.shard_map(
        local,
        mesh=mesh,
        in_specs=placed,
        out_specs=(P("ha", "dev", None, None), P(), P(), P(None, None, None, None, "ha")),
        check_vma=False,
    )
```
